32 devices in a mesh: panel: 4 (over y, x), front: 8 (over z, core).
Axes of the slice: x: 2, y: 2, z: 4, core: 2. Of those that a mesh axis runs over, the one named last changes fastest.
Arguments:
- top_source: bfloat16 [4, 128, 4096], P('panel', None, 'front'), may hold values from -6 to 6
- leaf_source: bfloat16 [4, 128, 73728], P('panel', None, 'front'), may hold values from -6 to 6
- top_inverse: bfloat16 [4, 4096, 4096], P('panel', 'front'), may hold values from -1 to 4
- leaf_inverse: bfloat16 [4, 288, 256, 256], P('panel', 'front'), may hold values from -1 to 4
- boundary: bfloat16 [4, 288, 128, 256], P('panel', 'front'), may hold values from -0.09375 to 0.09375
- touch_rows: int32 [4, 288, 128], P('panel', 'front'), may hold values from 0 to 4095, as said below
- coupling: float32 [4, 4096], P('panel', 'front'), may hold values from 0.3 to 1
Outputs:
- top_field: bfloat16 [4, 128, 4096], P('panel', None, 'front')
- leaf_field: bfloat16 [4, 128, 73728], P('panel', None, 'front')
The draws below stay inside these ranges and needn't reach their ends.
Inputs may be any that keep to these rules, and one draw needn't show every extreme that they name: `touch_rows`: front index d owns top front rows d * 512 to (d + 1) * 512 - 1; leaf j of a panel touches only rows owned by front indices j // 36 - 1, j // 36 and j // 36 + 1.
All inputs are finite; a program needn't handle non-finite values.
Results may differ from the reference program's by a relative error of at most 0.02.
Values may be sent and summed in bfloat16 or wider, within the bound.
No kernel may reach another device: no remote copies, remote signals or barrier semaphores. Data moves between devices by JAX's collectives and lax.ppermute only.
A program may use at most 64 MiB of HBM per device.

```python
import math
import jax
import jax.numpy as jnp
from jax import lax

TOP_WIDTH = 4096
LEAF_WIDTH = 256
EDGE_ROWS = 128
LEAVES = 36
SOURCES = 128
PANELS = 4
LEAVES_ALL = 288


def dominant(key, blocks, matrix_order):
    diag_key, off_key = jax.random.split(key)
    diagonal = jnp.exp(jax.random.uniform(diag_key, (blocks, matrix_order), jnp.float32, -0.7, 0.7))
    spread = jax.random.truncated_normal(off_key, -4.0, 4.0, (blocks, matrix_order, matrix_order), jnp.float32) * (0.5 / matrix_order ** 0.5)
    same_cell = lax.broadcasted_iota(jnp.int32, (matrix_order, matrix_order), 0) == lax.broadcasted_iota(jnp.int32, (matrix_order, matrix_order), 1)
    return jnp.where(same_cell[None], diagonal[:, :, None], spread)


def draw_top_inverse(key, part):
    folded = jax.random.fold_in(key, 11)
    return dominant(folded, PANELS, TOP_WIDTH).astype(jnp.bfloat16)


def draw_leaf_inverse(key, part):
    folded = jax.random.fold_in(key, 23)
    blocks = dominant(folded, PANELS * LEAVES_ALL, LEAF_WIDTH)
    return blocks.reshape(PANELS, LEAVES_ALL, LEAF_WIDTH, LEAF_WIDTH).astype(jnp.bfloat16)


def draw_touch_rows(key, part):
    folded = jax.random.fold_in(key, 37)
    shard_rows = TOP_WIDTH * LEAVES // LEAVES_ALL
    shape = (PANELS, LEAVES_ALL, EDGE_ROWS)
    leaf_ids = lax.broadcasted_iota(jnp.int32, shape, 1)
    edge_ids = lax.broadcasted_iota(jnp.int32, shape, 2)
    owner = leaf_ids // LEAVES
    centre = owner * shard_rows + leaf_ids % LEAVES * shard_rows // LEAVES
    offsets = jax.random.randint(folded, shape, -shard_rows, shard_rows, dtype=jnp.int32)
    offsets = jnp.where(edge_ids == 0, 0, offsets)
    return jnp.clip(centre + offsets, 0, TOP_WIDTH - 1).astype(jnp.int32)


def shard_levels(key, dims, cuts, low, top_value):
    loudness, own = 1.0, jax.random.fold_in(key, 6)
    for dim, blocks in cuts:
        steps = jnp.exp(jax.random.uniform(jax.random.fold_in(own, dim), (blocks,), jnp.float32, low / len(cuts), top_value / len(cuts)))
        loudness = loudness * jnp.repeat(steps, dims[dim] // blocks).reshape([-1 if axis == dim else 1 for axis in range(len(dims))])
    return loudness


def normal_values(rng, dims, width, reach, pieces=(), kind=jnp.bfloat16):
    entries = width * jax.random.normal(rng, dims, jnp.float32)
    if pieces:
        entries = entries * shard_levels(rng, dims, pieces, -0.22, 0.18)
    return jnp.clip(entries, -reach, reach).astype(kind)


def setup_inputs(seed: int = 0) -> dict:
    key_of = jax.random.split(jax.random.key(seed), 8)
    return {
        "top_source": normal_values(key_of[0], (PANELS, SOURCES, TOP_WIDTH), 1.0, 6.0, ((0, 4), (2, 8))),
        "leaf_source": normal_values(key_of[1], (PANELS, SOURCES, LEAVES_ALL * LEAF_WIDTH), 1.0, 6.0, ((0, 4), (2, 8))),
        "top_inverse": draw_top_inverse(jax.random.fold_in(key_of[7], 71), 0),
        "leaf_inverse": draw_leaf_inverse(jax.random.fold_in(key_of[7], 71), 0),
        "boundary": normal_values(key_of[4], (PANELS, LEAVES_ALL, EDGE_ROWS, LEAF_WIDTH), (16 * LEAF_WIDTH) ** -0.5, 0.09375, ((0, 4), (1, 8))),
        "touch_rows": draw_touch_rows(jax.random.fold_in(key_of[7], 71), 0),
        "coupling": jnp.clip(jnp.exp(math.log(1.0) - 1.2039728 * jax.random.uniform(key_of[6], (PANELS, TOP_WIDTH), jnp.float32) ** shard_levels(key_of[6], (PANELS, TOP_WIDTH), ((0, 4), (1, 8)), -0.2, 0.2)), 0.3, 1.0),
    }


def leaf_apply(inverse_blocks, vectors):
    return jnp.einsum("jab,sjb->sja", inverse_blocks.astype(jnp.float32), vectors.astype(jnp.float32))


def lift_rows(boundary_rows, picked):
    return jnp.einsum("jkb,sjk->sjb", boundary_rows.astype(jnp.float32), picked.astype(jnp.float32))


def reference(top_source, leaf_source, top_inverse, leaf_inverse, boundary, touch_rows, coupling):
    previous = jnp.zeros((SOURCES, TOP_WIDTH), jnp.bfloat16)
    forward_tops = []
    forward_leaves = []
    for panel_index in range(PANELS):
        flat_rows = touch_rows[panel_index].reshape(-1).astype(jnp.int32)
        vectors = leaf_source[panel_index].reshape(SOURCES, LEAVES_ALL, LEAF_WIDTH)
        interior = leaf_apply(leaf_inverse[panel_index], vectors).astype(jnp.bfloat16)
        pushed = jnp.einsum("jkb,sjb->sjk", boundary[panel_index].astype(jnp.float32), interior.astype(jnp.float32))
        gathered = jnp.zeros((SOURCES, TOP_WIDTH), jnp.float32).at[:, flat_rows].add(pushed.reshape(SOURCES, -1))
        rhs_rows = (top_source[panel_index].astype(jnp.float32) + coupling[panel_index] * previous.astype(jnp.float32) - gathered).astype(jnp.bfloat16)
        solved = jnp.dot(rhs_rows, top_inverse[panel_index].T, preferred_element_type=jnp.float32).astype(jnp.bfloat16)
        picked = solved[:, flat_rows].reshape(SOURCES, LEAVES_ALL, EDGE_ROWS)
        lifted = lift_rows(boundary[panel_index], picked).astype(jnp.bfloat16)
        leaf_out = (interior.astype(jnp.float32) - leaf_apply(leaf_inverse[panel_index], lifted)).astype(jnp.bfloat16)
        forward_tops.append(solved)
        forward_leaves.append(leaf_out)
        previous = solved
    arriving = jnp.zeros((SOURCES, TOP_WIDTH), jnp.bfloat16)
    top_final = [None] * PANELS
    leaf_final = [None] * PANELS
    for panel_index in reversed(range(PANELS)):
        flat_rows = touch_rows[panel_index].reshape(-1).astype(jnp.int32)
        correction = jnp.dot(arriving, top_inverse[panel_index].T, preferred_element_type=jnp.float32).astype(jnp.bfloat16)
        top_out = (forward_tops[panel_index].astype(jnp.float32) + correction.astype(jnp.float32)).astype(jnp.bfloat16)
        picked = correction[:, flat_rows].reshape(SOURCES, LEAVES_ALL, EDGE_ROWS)
        raised = lift_rows(boundary[panel_index], picked).astype(jnp.bfloat16)
        leaf_out = (forward_leaves[panel_index].astype(jnp.float32) - leaf_apply(leaf_inverse[panel_index], raised)).astype(jnp.bfloat16)
        top_final[panel_index] = top_out
        leaf_final[panel_index] = leaf_out.reshape(SOURCES, LEAVES_ALL * LEAF_WIDTH)
        arriving = (coupling[panel_index] * top_out.astype(jnp.float32)).astype(jnp.bfloat16)
    return jnp.stack(top_final), jnp.stack(leaf_final)
```

```python
import functools

import jax
import jax.numpy as jnp
from jax import lax
from jax.experimental import pallas as pl
from jax.experimental.pallas import tpu as pltpu
from jax.sharding import PartitionSpec as P

WAVES = 2
F32 = jnp.float32
BF16 = jnp.bfloat16
VMEM = pl.BlockSpec(memory_space=pltpu.VMEM)
SMEM = pl.BlockSpec(memory_space=pltpu.SMEM)


def params(mib):
    return pltpu.CompilerParams(vmem_limit_bytes=mib * 1024 * 1024)


def rows_dot(left, right):
    return lax.dot_general(left, right, (((1,), (1,)), ((), ())), preferred_element_type=F32)


def group_of(leaf_count):
    return max(g for g in (4, 3, 2, 1) if leaf_count % g == 0)


def push_kernel(group, source_ref, inverse_ref, boundary_ref, rows_ref, out_ref):
    leaf_size = inverse_ref.shape[2]
    edge = boundary_ref.shape[1]
    window = out_ref.shape[1]

    @pl.when(pl.program_id(0) == 0)
    def _():
        out_ref[...] = jnp.zeros_like(out_ref)

    columns = jnp.transpose(rows_ref[0])
    places = lax.broadcasted_iota(jnp.int32, (edge, window), 1)
    pushed, picks = [], []
    for g in range(group):
        vectors = source_ref[:, g * leaf_size : (g + 1) * leaf_size]
        interior = rows_dot(vectors, inverse_ref[g]).astype(BF16)
        pushed.append(rows_dot(interior, boundary_ref[g]).astype(BF16))
        picks.append(jnp.where(columns[:, g : g + 1] == places, 1.0, 0.0).astype(BF16))
    out_ref[...] += jnp.dot(
        jnp.concatenate(pushed, axis=1), jnp.concatenate(picks, axis=0), preferred_element_type=F32
    )


def lift_kernel(group, window_ref, source_ref, inverse_ref, boundary_ref, rows_ref, out_ref):
    leaf_size = inverse_ref.shape[2]
    edge = boundary_ref.shape[1]
    window = window_ref.shape[1]
    places = lax.broadcasted_iota(jnp.int32, (window, edge), 0)
    picks = [
        jnp.where(rows_ref[0][g : g + 1, :] == places, 1.0, 0.0).astype(BF16) for g in range(group)
    ]
    picked = jnp.dot(
        window_ref[...], jnp.concatenate(picks, axis=1), preferred_element_type=F32
    ).astype(BF16)
    for g in range(group):
        lifted = jnp.dot(
            picked[:, g * edge : (g + 1) * edge], boundary_ref[g], preferred_element_type=F32
        )
        here = slice(g * leaf_size, (g + 1) * leaf_size)
        vectors = (source_ref[:, here].astype(F32) - lifted).astype(BF16)
        out_ref[:, here] = rows_dot(vectors, inverse_ref[g]).astype(BF16)


def fold_kernel(blocks, first, meta_ref, inverse_ref, *refs):
    base_refs = refs[:blocks]
    in_refs = () if first else refs[blocks : 2 * blocks]
    out_ref = refs[-1]
    wave_rows, rows = out_ref.shape
    here = pl.ds(pl.multiple_of(meta_ref[1] * wave_rows, wave_rows), wave_rows)
    forward = meta_ref[0] == 1
    fed = meta_ref[2] == 1
    total = jnp.zeros((wave_rows, rows), F32)
    for i in range(blocks):
        if first:
            vectors = base_refs[i][here, :]
        else:
            base = jnp.where(forward, base_refs[i][here, :].astype(F32), 0.0)
            vectors = (jnp.where(fed, in_refs[i][...].astype(F32), 0.0) + base).astype(BF16)
        place = pl.ds(pl.multiple_of(meta_ref[3 + i] * rows, rows), rows)
        total += jnp.dot(vectors, inverse_ref[place, :], preferred_element_type=F32)
    out_ref[...] = total.astype(BF16)


def join_kernel(meta_ref, mine_ref, other_ref, state_ref, scale_ref, next_ref, out_ref):
    wave_rows = mine_ref.shape[0]
    here = pl.ds(pl.multiple_of(meta_ref[1] * wave_rows, wave_rows), wave_rows)
    mode = meta_ref[0]
    solved = (mine_ref[...].astype(F32) + other_ref[...].astype(F32)).astype(BF16).astype(F32)
    older = state_ref[here, :].astype(F32)
    field = (solved + jnp.where(mode == 2, older, 0.0)).astype(BF16)
    scale = scale_ref[pl.ds(jnp.where(mode == 2, 1, 0), 1), :]
    out_ref[...] = (scale * field.astype(F32)).astype(BF16)
    next_ref[...] = state_ref[...]

    @pl.when(mode > 0)
    def _():
        next_ref[here, :] = field


def turn_routes(turn, panels, waves):
    at = [s if s < panels else 2 * (panels - 1) - s for s in range(2 * panels - 1)]
    pairs = []
    for wave in range(waves):
        step = turn - wave
        if 0 <= step < 2 * (panels - 1):
            pairs.append((at[step], at[step + 1]))
    sources = [a for a, _ in pairs]
    targets = [b for _, b in pairs]
    for panel in range(panels):
        if panel not in sources and panel not in targets:
            pairs.append((panel, panel))
    spare = [p for p in targets if p not in sources]
    unfed = [p for p in sources if p not in targets]
    return pairs + list(zip(spare, unfed))


def spread(values, panel_pairs, chips):
    half = chips // 2
    received = []
    for i in range(half):
        route = []
        for start, end in panel_pairs:
            for chip in range(chips):
                for core in range(2):
                    there = chip ^ (core * half + i)
                    route.append(
                        (2 * (start * chips + chip) + core, 2 * (end * chips + there) + core)
                    )
        received.append(lax.ppermute(values, ("panel", "front"), route))
    return received


def body(top_source, leaf_source, top_inverse, leaf_inverse, boundary, touch_rows, coupling):
    sources = top_source.shape[1]
    rows = top_source.shape[2]
    width = top_inverse.shape[2]
    leaf_count, leaf_size = leaf_inverse.shape[1:3]
    edge = boundary.shape[2]
    panels = lax.axis_size("panel")
    front = lax.axis_size("front")
    chips, half = front // 2, front // 4
    chip_rows = 2 * rows
    panel = lax.axis_index("panel")
    place = lax.axis_index("front")
    chip, core = place // 2, place % 2
    wave_rows = sources // WAVES
    group = group_of(leaf_count)
    steps = leaf_count // group

    swap_core = [(i, i ^ 1) for i in range(front)]
    swap_chip = [(i, i + 1) for i in range(1, front - 1, 2)]
    swap_chip = swap_chip + [(j, i) for i, j in swap_chip]

    own_half = (chip // half) ^ core
    kept = lax.dynamic_slice_in_dim(top_inverse[0], own_half * (width // 2), width // 2, 1)
    given = lax.dynamic_slice_in_dim(top_inverse[0], (1 - own_half) * (width // 2), width // 2, 1)
    taken = lax.ppermute(given, "front", swap_core)
    low = jnp.where(core == 0, kept, taken)
    high = jnp.where(core == 0, taken, kept)
    inverse = jnp.concatenate([low.T, high.T], axis=1)

    local_rows = touch_rows[0] - (place - 1) * rows
    grouped = local_rows.reshape(steps, group, edge)
    padded = jnp.concatenate([grouped, jnp.zeros((steps, 8 - group, edge), jnp.int32)], axis=1)
    leaf_specs = [
        pl.BlockSpec((sources, group * leaf_size), lambda i: (0, i)),
        pl.BlockSpec((group, leaf_size, leaf_size), lambda i: (i, 0, 0)),
        pl.BlockSpec((group, edge, leaf_size), lambda i: (i, 0, 0)),
        pl.BlockSpec((1, 8, edge), lambda i: (i, 0, 0)),
    ]
    leaf_args = (leaf_source[0], leaf_inverse[0], boundary[0], padded)
    windows = pl.pallas_call(
        functools.partial(push_kernel, group),
        grid=(steps,),
        out_shape=jax.ShapeDtypeStruct((sources, 3 * rows), F32),
        in_specs=leaf_specs,
        out_specs=pl.BlockSpec((sources, 3 * rows), lambda i: (0, 0)),
        compiler_params=params(40),
    )(*leaf_args)
    outward = jnp.where(core == 0, windows[:, :rows], windows[:, 2 * rows :]).astype(BF16)
    inward = lax.ppermute(outward, "front", swap_chip)
    chip_part = jnp.where(core == 0, windows[:, rows:], windows[:, :chip_rows])
    own_part = top_source[0].astype(F32) - inward.astype(F32)
    blank = jnp.zeros_like(own_part)
    own_part = jnp.where(
        core == 0,
        jnp.concatenate([own_part, blank], axis=1),
        jnp.concatenate([blank, own_part], axis=1),
    )
    partial = (own_part - chip_part).astype(BF16)
    partner = lax.ppermute(partial, "front", swap_core)
    known = (partial.astype(F32) + partner.astype(F32)).astype(BF16)
    base = spread(known, [(p, p) for p in range(panels)], chips)

    mine = coupling
    later = lax.ppermute(mine, "panel", [((p + 1) % panels, p) for p in range(panels)])
    forward_scale = jnp.where(panel == panels - 1, mine, later)
    scales = jnp.concatenate([forward_scale, mine], axis=0)
    partner_scales = lax.ppermute(scales, "front", swap_core)
    scales = jnp.where(
        core == 0,
        jnp.concatenate([scales, partner_scales], axis=1),
        jnp.concatenate([partner_scales, scales], axis=1),
    )
    offsets = [(chip % half) ^ i for i in range(half)]
    state = jnp.zeros((sources, chip_rows), BF16)
    turns = 2 * (panels - 1) + WAVES
    arrived = []
    for turn in range(turns):
        up_wave = turn - panel
        down_wave = turn - (2 * (panels - 1) - panel)
        up = (up_wave >= 0) & (up_wave < WAVES)
        down = (down_wave >= 0) & (down_wave < WAVES) & (panel < panels - 1)
        mode = jnp.where(up, 1, jnp.where(down, 2, 0))
        wave = jnp.where(up, up_wave, jnp.where(down, down_wave, 0))
        fed = jnp.where((panel == 0) & up, 0, 1)
        meta = jnp.stack([mode, wave, fed] + offsets).astype(jnp.int32)
        first = turn == 0
        share = pl.pallas_call(
            functools.partial(fold_kernel, half, first),
            out_shape=jax.ShapeDtypeStruct((wave_rows, chip_rows), BF16),
            in_specs=[SMEM] + [VMEM] * (1 + half + len(arrived)),
            out_specs=VMEM,
            compiler_params=params(32),
        )(meta, inverse, *base, *arrived)
        other = lax.ppermute(share, "front", swap_core)
        state, outgoing = pl.pallas_call(
            join_kernel,
            out_shape=(
                jax.ShapeDtypeStruct((sources, chip_rows), BF16),
                jax.ShapeDtypeStruct((wave_rows, chip_rows), BF16),
            ),
            in_specs=[SMEM] + [VMEM] * 4,
            out_specs=(VMEM, VMEM),
            compiler_params=params(32),
        )(meta, share, other, state, scales)
        if turn < turns - 1:
            arrived = spread(outgoing, turn_routes(turn, panels, WAVES), chips)

    top_field = jnp.where(core == 0, state[:, :rows], state[:, rows:])
    beside = lax.ppermute(top_field, "front", swap_chip)
    window = jnp.where(
        core == 0,
        jnp.concatenate([beside, state], axis=1),
        jnp.concatenate([state, beside], axis=1),
    )
    leaf_field = pl.pallas_call(
        functools.partial(lift_kernel, group),
        grid=(steps,),
        out_shape=jax.ShapeDtypeStruct((sources, leaf_count * leaf_size), BF16),
        in_specs=[pl.BlockSpec((sources, 3 * rows), lambda i: (0, 0))] + leaf_specs,
        out_specs=pl.BlockSpec((sources, group * leaf_size), lambda i: (0, i)),
        compiler_params=params(40),
    )(window, *leaf_args)
    return (top_field[None], leaf_field[None])


def solution(mesh):
    placed = (
        P("panel", None, "front"),
        P("panel", None, "front"),
        P("panel", "front", None),
        P("panel", "front", None, None),
        P("panel", "front", None, None),
        P("panel", "front", None),
        P("panel", "front"),
    )
    return jax.shard_map(
        body,
        mesh=mesh,
        in_specs=placed,
        out_specs=(P("panel", None, "front"), P("panel", None, "front")),
        check_vma=False,
    )
```

```python
import functools

import jax
import jax.numpy as jnp
from jax import lax
from jax.experimental import pallas as pl
from jax.experimental.pallas import tpu as pltpu
from jax.sharding import PartitionSpec as P

WAVES = 2
F32 = jnp.float32
BF16 = jnp.bfloat16
VMEM = pl.BlockSpec(memory_space=pltpu.VMEM)
SMEM = pl.BlockSpec(memory_space=pltpu.SMEM)
ANY = pl.BlockSpec(memory_space=pl.ANY)


def params(mib):
    return pltpu.CompilerParams(vmem_limit_bytes=mib * 1024 * 1024)


def in_vmem(value):
    return pltpu.with_memory_space_constraint(value, pltpu.VMEM)


def in_hbm(value):
    return pltpu.with_memory_space_constraint(value, pltpu.HBM)


def rows_dot(left, right):
    return lax.dot_general(left, right, (((1,), (1,)), ((), ())), preferred_element_type=F32)


def group_of(leaf_count, most):
    return max(g for g in range(1, most + 1) if leaf_count % g == 0)


def push_kernel(
    group,
    meta_ref,
    rows_ref,
    source_hbm,
    inverse_hbm,
    boundary_hbm,
    out_ref,
    interior_ref,
    inverse_ref,
    boundary_ref,
    source_ref,
    pick_ref,
    sems,
):
    leaf_count, leaf_size = inverse_ref.shape[:2]
    edge = boundary_ref.shape[1]
    window = out_ref.shape[1]
    copies = []
    for step in range(leaf_count // group):
        leaves = pl.ds(step * group, group)
        lanes = pl.ds(step * group * leaf_size, group * leaf_size)
        parts = (
            (source_hbm.at[:, lanes], source_ref.at[:, lanes]),
            (inverse_hbm.at[leaves], inverse_ref.at[leaves]),
            (boundary_hbm.at[leaves], boundary_ref.at[leaves]),
        )
        copies.append(
            [pltpu.make_async_copy(a, b, sems.at[step, i]) for i, (a, b) in enumerate(parts)]
        )
        for copy in copies[-1]:
            copy.start()
    local = rows_ref[...] - meta_ref[0, 0]
    spare = -leaf_count % 8
    if spare:
        local = jnp.concatenate([local, jnp.zeros((spare, edge), jnp.int32)], axis=0)
    columns = jnp.transpose(local).astype(jnp.int16)
    places = lax.broadcasted_iota(jnp.int16, (edge, window), 1)
    for step in range(leaf_count // group):
        for copy in copies[step]:
            copy.wait()
        first = step * group
        for g in range(group):
            pick_ref[step % 2, g * edge : (g + 1) * edge, :] = jnp.where(
                columns[:, first + g : first + g + 1] == places, jnp.bfloat16(1), jnp.bfloat16(0)
            )
        interior = []
        for j in range(first, first + group):
            lanes = slice(j * leaf_size, (j + 1) * leaf_size)
            interior.append(rows_dot(source_ref[:, lanes], inverse_ref[j]).astype(BF16))
            interior_ref[:, lanes] = interior[-1]
        pushed = [
            rows_dot(interior[g], boundary_ref[first + g]).astype(BF16) for g in range(group)
        ]
        total = jnp.dot(
            jnp.concatenate(pushed, axis=1), pick_ref[step % 2], preferred_element_type=F32
        )
        if step == 0:
            out_ref[...] = total
        else:
            out_ref[...] += total


def pick_kernel(meta_ref, rows_ref, out_ref):
    leaf_count, edge = rows_ref.shape
    window = out_ref.shape[0]
    local = (rows_ref[...] - meta_ref[0, 0]).astype(jnp.int16)
    places = lax.broadcasted_iota(jnp.int16, (window, edge), 0)
    for j in range(leaf_count):
        out_ref[:, j * edge : (j + 1) * edge] = jnp.where(
            local[j : j + 1, :] == places, jnp.bfloat16(1), jnp.bfloat16(0)
        )


def lift_matrix_kernel(inverse_ref, boundary_ref, out_ref):
    leaf_count, edge, leaf_size = boundary_ref.shape
    for j in range(leaf_count):
        out_ref[j] = rows_dot(boundary_ref[j], inverse_ref[j]).astype(BF16)


def leaf_kernel(group, window_ref, pick_ref, matrix_ref, interior_ref, out_hbm, out_ref, sems):
    leaf_count, edge, leaf_size = matrix_ref.shape
    window = window_ref[...]
    copies = []
    for step in range(leaf_count // group):
        first = step * group
        picked = jnp.dot(
            window,
            pick_ref[:, first * edge : (first + group) * edge],
            preferred_element_type=F32,
        ).astype(BF16)
        for g in range(group):
            lanes = slice((first + g) * leaf_size, (first + g + 1) * leaf_size)
            lifted = jnp.dot(
                picked[:, g * edge : (g + 1) * edge],
                matrix_ref[first + g],
                preferred_element_type=F32,
            )
            out_ref[:, lanes] = (interior_ref[:, lanes].astype(F32) - lifted).astype(BF16)
        lanes = pl.ds(first * leaf_size, group * leaf_size)
        copies.append(
            pltpu.make_async_copy(out_ref.at[:, lanes], out_hbm.at[:, lanes], sems.at[step])
        )
        copies[-1].start()
    for copy in copies:
        copy.wait()


def half_kernel(meta_ref, inverse_hbm, out_ref, sem):
    columns = out_ref.shape[1]
    start = pl.multiple_of((1 - meta_ref[0, 1]) * columns, columns)
    copy = pltpu.make_async_copy(inverse_hbm.at[:, pl.ds(start, columns)], out_ref, sem)
    copy.start()
    copy.wait()


def turn_kernel(meta_ref, inverse_hbm, taken_ref, out_ref, kept_ref, sem):
    columns, rows = out_ref.shape[0], taken_ref.shape[0]
    start = pl.multiple_of(meta_ref[0, 1] * columns, columns)
    copy = pltpu.make_async_copy(inverse_hbm.at[:, pl.ds(start, columns)], kept_ref, sem)
    copy.start()
    copy.wait()
    piece = min(columns, 256)
    for k in range(0, columns, piece):
        kept = jnp.transpose(kept_ref[:, k : k + piece])
        taken = jnp.transpose(taken_ref[:, k : k + piece])

        @pl.when(meta_ref[0, 2] == 0)
        def _():
            out_ref[k : k + piece, :rows] = kept
            out_ref[k : k + piece, rows:] = taken

        @pl.when(meta_ref[0, 2] != 0)
        def _():
            out_ref[k : k + piece, :rows] = taken
            out_ref[k : k + piece, rows:] = kept


def fold_kernel(turn, blocks, meta_ref, inverse_ref, *refs):
    base_refs = refs[:blocks]
    in_refs = refs[blocks : 2 * blocks] if turn else ()
    out_ref = refs[-1]
    wave_rows, rows = out_ref.shape
    here = pl.ds(pl.multiple_of(meta_ref[turn + 1, 1] * wave_rows, wave_rows), wave_rows)
    forward = meta_ref[turn + 1, 0] == 1
    fed = meta_ref[turn + 1, 2] == 1
    total = jnp.zeros((wave_rows, rows), F32)
    for i in range(blocks):
        if turn:
            base = jnp.where(forward, base_refs[i][here, :].astype(F32), 0.0)
            vectors = (jnp.where(fed, in_refs[i][...].astype(F32), 0.0) + base).astype(BF16)
        else:
            vectors = base_refs[i][here, :]
        place = pl.ds(pl.multiple_of(meta_ref[0, 3 + i] * rows, rows), rows)
        total += jnp.dot(vectors, inverse_ref[place, :], preferred_element_type=F32)
    out_ref[...] = total.astype(BF16)


def join_kernel(turn, meta_ref, mine_ref, other_ref, state_ref, scale_ref, next_ref, out_ref):
    wave_rows = mine_ref.shape[0]
    here = pl.ds(pl.multiple_of(meta_ref[turn + 1, 1] * wave_rows, wave_rows), wave_rows)
    mode = meta_ref[turn + 1, 0]
    solved = (mine_ref[...].astype(F32) + other_ref[...].astype(F32)).astype(BF16).astype(F32)
    older = state_ref[here, :].astype(F32)
    field = (solved + jnp.where(mode == 2, older, 0.0)).astype(BF16)
    scale = scale_ref[pl.ds(jnp.where(mode == 2, 1, 0), 1), :]
    out_ref[...] = (scale * field.astype(F32)).astype(BF16)

    @pl.when(mode > 0)
    def _():
        next_ref[here, :] = field


def turn_routes(turn, panels, waves):
    at = [s if s < panels else 2 * (panels - 1) - s for s in range(2 * panels - 1)]
    pairs = []
    for wave in range(waves):
        step = turn - wave
        if 0 <= step < 2 * (panels - 1):
            pairs.append((at[step], at[step + 1]))
    sources = [a for a, _ in pairs]
    targets = [b for _, b in pairs]
    for panel in range(panels):
        if panel not in sources and panel not in targets:
            pairs.append((panel, panel))
    spare = [p for p in targets if p not in sources]
    unfed = [p for p in sources if p not in targets]
    return pairs + list(zip(spare, unfed))


def spread(values, panel_pairs, chips):
    half = chips // 2
    received = []
    for i in range(half):
        route = []
        for start, end in panel_pairs:
            for chip in range(chips):
                for core in range(2):
                    there = chip ^ (core * half + i)
                    route.append(
                        (2 * (start * chips + chip) + core, 2 * (end * chips + there) + core)
                    )
        received.append(lax.ppermute(values, ("panel", "front"), route))
    return received


def schedule(panels, half, panel, place, rows):
    chip, core = place // 2, place % 2
    table = [[(place - 1) * rows, (chip // half) ^ core, core] + [(chip % half) ^ i for i in range(half)]]
    for turn in range(2 * (panels - 1) + WAVES):
        up_wave = turn - panel
        down_wave = turn - (2 * (panels - 1) - panel)
        up = (up_wave >= 0) & (up_wave < WAVES)
        down = (down_wave >= 0) & (down_wave < WAVES) & (panel < panels - 1)
        table.append(
            [
                jnp.where(up, 1, jnp.where(down, 2, 0)),
                jnp.where(up, up_wave, jnp.where(down, down_wave, 0)),
                jnp.where((panel == 0) & up, 0, 1),
            ]
            + [0] * half
        )
    return jnp.stack([jnp.stack([jnp.asarray(v, jnp.int32) for v in row]) for row in table])


def body(top_source, leaf_source, top_inverse, leaf_inverse, boundary, touch_rows, coupling):
    sources = top_source.shape[1]
    rows = top_source.shape[2]
    width = top_inverse.shape[2]
    leaf_count, leaf_size = leaf_inverse.shape[1:3]
    edge = boundary.shape[2]
    panels = lax.axis_size("panel")
    front = lax.axis_size("front")
    chips, half = front // 2, front // 4
    chip_rows = 2 * rows
    panel = lax.axis_index("panel")
    place = lax.axis_index("front")
    core = place % 2
    wave_rows = sources // WAVES
    group = group_of(leaf_count, 6)
    steps = leaf_count // group
    all_lanes = leaf_count * leaf_size
    meta = schedule(panels, half, panel, place, rows)

    swap_core = [(i, i ^ 1) for i in range(front)]
    swap_chip = [(i, i + 1) for i in range(1, front - 1, 2)]
    swap_chip = swap_chip + [(j, i) for i, j in swap_chip]

    windows, interior, inverse_here, boundary_here = pl.pallas_call(
        functools.partial(push_kernel, group),
        out_shape=(
            pltpu.VMEM((sources, 3 * rows), F32),
            pltpu.VMEM((sources, all_lanes), BF16),
            pltpu.VMEM((leaf_count, leaf_size, leaf_size), BF16),
            pltpu.VMEM((leaf_count, edge, leaf_size), BF16),
        ),
        in_specs=[SMEM, VMEM, ANY, ANY, ANY],
        out_specs=(VMEM, VMEM, VMEM, VMEM),
        scratch_shapes=[
            pltpu.VMEM((sources, all_lanes), BF16),
            pltpu.VMEM((2, group * edge, 3 * rows), BF16),
            pltpu.SemaphoreType.DMA((steps, 3)),
        ],
        compiler_params=params(20),
    )(meta, touch_rows[0], in_hbm(leaf_source[0]), in_hbm(leaf_inverse[0]), in_hbm(boundary[0]))
    outward = jnp.where(core == 0, windows[:, :rows], windows[:, 2 * rows :]).astype(BF16)
    inward = lax.ppermute(outward, "front", swap_chip)
    chip_part = jnp.where(core == 0, windows[:, rows:], windows[:, :chip_rows])
    own_part = top_source[0].astype(F32) - inward.astype(F32)
    blank = jnp.zeros_like(own_part)
    own_part = jnp.where(
        core == 0,
        jnp.concatenate([own_part, blank], axis=1),
        jnp.concatenate([blank, own_part], axis=1),
    )
    partial = (own_part - chip_part).astype(BF16)
    partner = lax.ppermute(partial, "front", swap_core)
    known = (partial.astype(F32) + partner.astype(F32)).astype(BF16)
    base = [in_vmem(b) for b in spread(known, [(p, p) for p in range(panels)], chips)]

    given = pl.pallas_call(
        half_kernel,
        out_shape=pltpu.VMEM((rows, width // 2), BF16),
        in_specs=[SMEM, ANY],
        out_specs=VMEM,
        scratch_shapes=[pltpu.SemaphoreType.DMA],
        compiler_params=params(4),
    )(meta, in_hbm(top_inverse[0]))
    taken = lax.ppermute(given, "front", swap_core)
    inverse = pl.pallas_call(
        turn_kernel,
        out_shape=pltpu.VMEM((width // 2, chip_rows), BF16),
        in_specs=[SMEM, ANY, VMEM],
        out_specs=VMEM,
        scratch_shapes=[pltpu.VMEM((rows, width // 2), BF16), pltpu.SemaphoreType.DMA],
        compiler_params=params(8),
    )(meta, in_hbm(top_inverse[0]), in_vmem(taken))
    inverse = in_vmem(inverse)

    later = lax.ppermute(coupling, "panel", [((p + 1) % panels, p) for p in range(panels)])
    forward_scale = jnp.where(panel == panels - 1, coupling, later)
    scales = jnp.concatenate([forward_scale, coupling], axis=0)
    partner_scales = lax.ppermute(scales, "front", swap_core)
    scales = jnp.where(
        core == 0,
        jnp.concatenate([scales, partner_scales], axis=1),
        jnp.concatenate([partner_scales, scales], axis=1),
    )
    scales = in_vmem(scales)
    state = jnp.zeros((sources, chip_rows), BF16)
    turns = 2 * (panels - 1) + WAVES
    arrived = []
    for turn in range(turns):
        share = pl.pallas_call(
            functools.partial(fold_kernel, turn, half),
            out_shape=pltpu.VMEM((wave_rows, chip_rows), BF16),
            in_specs=[SMEM] + [VMEM] * (1 + half + len(arrived)),
            out_specs=VMEM,
            compiler_params=params(4),
        )(meta, inverse, *base, *arrived)
        other = lax.ppermute(share, "front", swap_core)
        state, outgoing = pl.pallas_call(
            functools.partial(join_kernel, turn),
            out_shape=(
                pltpu.VMEM((sources, chip_rows), BF16),
                pltpu.VMEM((wave_rows, chip_rows), BF16),
            ),
            in_specs=[SMEM] + [VMEM] * 4,
            out_specs=(VMEM, VMEM),
            input_output_aliases={3: 0},
            compiler_params=params(4),
        )(meta, in_vmem(share), in_vmem(other), in_vmem(state), scales)
        if turn < turns - 1:
            routes = turn_routes(turn, panels, WAVES)
            arrived = [in_vmem(a) for a in spread(outgoing, routes, chips)]

    picks = pl.pallas_call(
        pick_kernel,
        out_shape=pltpu.VMEM((3 * rows, leaf_count * edge), BF16),
        in_specs=[SMEM, VMEM],
        out_specs=VMEM,
        compiler_params=params(4),
    )(meta, touch_rows[0])
    matrices = pl.pallas_call(
        lift_matrix_kernel,
        out_shape=pltpu.VMEM((leaf_count, edge, leaf_size), BF16),
        in_specs=[VMEM, VMEM],
        out_specs=VMEM,
        compiler_params=params(4),
    )(in_vmem(inverse_here), in_vmem(boundary_here))
    top_field = jnp.where(core == 0, state[:, :rows], state[:, rows:])
    beside = lax.ppermute(top_field, "front", swap_chip)
    window = jnp.where(
        core == 0,
        jnp.concatenate([beside, state], axis=1),
        jnp.concatenate([state, beside], axis=1),
    )
    leaf_field = pl.pallas_call(
        functools.partial(leaf_kernel, group),
        out_shape=jax.ShapeDtypeStruct((sources, all_lanes), BF16),
        in_specs=[VMEM] * 4,
        out_specs=ANY,
        scratch_shapes=[
            pltpu.VMEM((sources, all_lanes), BF16),
            pltpu.SemaphoreType.DMA((steps,)),
        ],
        compiler_params=params(8),
    )(in_vmem(window), in_vmem(picks), in_vmem(matrices), in_vmem(interior))
    return (top_field[None], leaf_field[None])


def solution(mesh):
    placed = (
        P("panel", None, "front"),
        P("panel", None, "front"),
        P("panel", "front", None),
        P("panel", "front", None, None),
        P("panel", "front", None, None),
        P("panel", "front", None),
        P("panel", "front"),
    )
    return jax.shard_map(
        body,
        mesh=mesh,
        in_specs=placed,
        out_specs=(P("panel", None, "front"), P("panel", None, "front")),
        check_vma=False,
    )
```

```python
import functools

import jax
import jax.numpy as jnp
from jax import lax
from jax.experimental import pallas as pl
from jax.experimental.pallas import tpu as pltpu
from jax.sharding import PartitionSpec as P

WAVES = 2
F32 = jnp.float32
BF16 = jnp.bfloat16
VMEM = pl.BlockSpec(memory_space=pltpu.VMEM)
ANY = pl.BlockSpec(memory_space=pl.ANY)


def params(mib):
    return pltpu.CompilerParams(vmem_limit_bytes=mib * 1024 * 1024)


def in_vmem(value):
    return pltpu.with_memory_space_constraint(value, pltpu.VMEM)


def in_hbm(value):
    return pltpu.with_memory_space_constraint(value, pltpu.HBM)


def rows_dot(left, right):
    return lax.dot_general(left, right, (((1,), (1,)), ((), ())), preferred_element_type=F32)


def group_of(leaf_count, most):
    return max(g for g in range(1, most + 1) if leaf_count % g == 0)


def own_place():
    place = lax.axis_index("front")
    return place // 2, place % 2


def own_turn(turn):
    panel = lax.axis_index("panel")
    panels = lax.axis_size("panel")
    up_wave = turn - panel
    down_wave = turn - (2 * (panels - 1) - panel)
    up = (up_wave >= 0) & (up_wave < WAVES)
    down = (down_wave >= 0) & (down_wave < WAVES) & (panel < panels - 1)
    wave = jnp.where(up, up_wave, jnp.where(down, down_wave, 0))
    return up, down, wave, (panel > 0) | down


def push_kernel(
    group,
    rows_ref,
    top_ref,
    source_hbm,
    inverse_hbm,
    boundary_hbm,
    outward_ref,
    partial_ref,
    interior_ref,
    source_ref,
    inverse_ref,
    boundary_ref,
    pick_ref,
    total_ref,
    sems,
):
    leaf_count, leaf_size = inverse_ref.shape[:2]
    edge = boundary_ref.shape[1]
    rows = top_ref.shape[1]
    window = 3 * rows
    copies = []
    for step in range(leaf_count // group):
        leaves = pl.ds(step * group, group)
        lanes = pl.ds(step * group * leaf_size, group * leaf_size)
        parts = (
            (source_hbm.at[:, lanes], source_ref.at[:, lanes]),
            (inverse_hbm.at[leaves], inverse_ref.at[leaves]),
            (boundary_hbm.at[leaves], boundary_ref.at[leaves]),
        )
        copies.append(
            [pltpu.make_async_copy(a, b, sems.at[step, i]) for i, (a, b) in enumerate(parts)]
        )
        for copy in copies[-1]:
            copy.start()
    local = rows_ref[...] - (lax.axis_index("front") - 1) * rows
    spare = -leaf_count % 8
    if spare:
        local = jnp.concatenate([local, jnp.zeros((spare, edge), jnp.int32)], axis=0)
    columns = jnp.transpose(local).astype(jnp.int16)
    places = lax.broadcasted_iota(jnp.int16, (edge, window), 1)
    for step in range(leaf_count // group):
        for copy in copies[step]:
            copy.wait()
        first = step * group
        for g in range(group):
            pick_ref[step % 2, g * edge : (g + 1) * edge, :] = jnp.where(
                columns[:, first + g : first + g + 1] == places, jnp.bfloat16(1), jnp.bfloat16(0)
            )
        interior = []
        for j in range(first, first + group):
            lanes = slice(j * leaf_size, (j + 1) * leaf_size)
            interior.append(rows_dot(source_ref[:, lanes], inverse_ref[j]).astype(BF16))
            interior_ref[:, lanes] = interior[-1]
        pushed = [
            rows_dot(interior[g], boundary_ref[first + g]).astype(BF16) for g in range(group)
        ]
        total = jnp.dot(
            jnp.concatenate(pushed, axis=1), pick_ref[step % 2], preferred_element_type=F32
        )
        if step == 0:
            total_ref[...] = total
        else:
            total_ref[...] += total
    core = own_place()[1]
    top = top_ref[...].astype(F32)

    @pl.when(core == 0)
    def _():
        outward_ref[...] = total_ref[:, :rows].astype(BF16)
        partial_ref[:, :rows] = top - total_ref[:, rows : 2 * rows]
        partial_ref[:, rows:] = -total_ref[:, 2 * rows :]

    @pl.when(core != 0)
    def _():
        outward_ref[...] = total_ref[:, 2 * rows :].astype(BF16)
        partial_ref[:, :rows] = -total_ref[:, :rows]
        partial_ref[:, rows:] = top - total_ref[:, rows : 2 * rows]


def pick_kernel(rows_ref, after_ref, out_ref):
    leaf_count, edge = rows_ref.shape
    window = out_ref.shape[0]
    rows = window // 3
    place = lax.axis_index("front")
    local = rows_ref[...] - (place - 1) * rows
    shifted = jnp.where(local < rows, local + 2 * rows, local - rows)
    local = jnp.where(place % 2 == 0, shifted, local).astype(jnp.int16)
    places = lax.broadcasted_iota(jnp.int16, (window, edge), 0)
    for j in range(leaf_count):
        out_ref[:, j * edge : (j + 1) * edge] = jnp.where(
            local[j : j + 1, :] == places, jnp.bfloat16(1), jnp.bfloat16(0)
        )


def lift_matrix_kernel(group, inverse_hbm, boundary_hbm, after_ref, out_ref, inverse_ref, boundary_ref, sems):
    leaf_count = out_ref.shape[0]
    copies = []
    for step in range(leaf_count // group):
        leaves = pl.ds(step * group, group)
        parts = (
            (inverse_hbm.at[leaves], inverse_ref.at[leaves]),
            (boundary_hbm.at[leaves], boundary_ref.at[leaves]),
        )
        copies.append(
            [pltpu.make_async_copy(a, b, sems.at[step, i]) for i, (a, b) in enumerate(parts)]
        )
        for copy in copies[-1]:
            copy.start()
    for step in range(leaf_count // group):
        for copy in copies[step]:
            copy.wait()
        for j in range(step * group, (step + 1) * group):
            out_ref[j] = rows_dot(boundary_ref[j], inverse_ref[j]).astype(BF16)


def near_kernel(state_ref, pick_ref, out_ref):
    out_ref[...] = jnp.dot(
        state_ref[...], pick_ref[: state_ref.shape[1], :], preferred_element_type=F32
    ).astype(BF16)


def leaf_kernel(
    group, beside_ref, picked_ref, pick_ref, matrix_ref, interior_ref, out_hbm, out_ref, sems
):
    leaf_count, edge, leaf_size = matrix_ref.shape
    rows = beside_ref.shape[1]
    beside = beside_ref[...]
    copies = []
    for step in range(leaf_count // group):
        first = step * group
        span = slice(first * edge, (first + group) * edge)
        picked = jnp.dot(beside, pick_ref[2 * rows :, span], preferred_element_type=F32)
        picked = (picked + picked_ref[:, span].astype(F32)).astype(BF16)
        for g in range(group):
            lanes = slice((first + g) * leaf_size, (first + g + 1) * leaf_size)
            lifted = jnp.dot(
                picked[:, g * edge : (g + 1) * edge],
                matrix_ref[first + g],
                preferred_element_type=F32,
            )
            out_ref[:, lanes] = (interior_ref[:, lanes].astype(F32) - lifted).astype(BF16)
        lanes = pl.ds(first * leaf_size, group * leaf_size)
        copies.append(
            pltpu.make_async_copy(out_ref.at[:, lanes], out_hbm.at[:, lanes], sems.at[step])
        )
        copies[-1].start()
    for copy in copies:
        copy.wait()


def half_copies(parity, inverse_hbm, to_ref, sems):
    pairs = sems.shape[0]
    span = to_ref.shape[1] // pairs
    copies = []
    for q in range(pairs):
        start = pl.multiple_of((2 * q + parity) * span, span)
        copies.append(
            pltpu.make_async_copy(
                inverse_hbm.at[:, pl.ds(start, span)],
                to_ref.at[:, pl.ds(q * span, span)],
                sems.at[q],
            )
        )
        copies[-1].start()
    return copies


def half_kernel(inverse_hbm, after_ref, out_ref, sems):
    chip, core = own_place()
    for copy in half_copies((chip + core + 1) % 2, inverse_hbm, out_ref, sems):
        copy.wait()


def turn_kernel(inverse_hbm, taken_ref, out_ref, kept_ref, sems):
    columns, rows = out_ref.shape[0], taken_ref.shape[0]
    chip, core = own_place()
    copies = half_copies((chip + core) % 2, inverse_hbm, kept_ref, sems)
    span = columns // len(copies)
    piece = min(span, 256)
    for q, copy in enumerate(copies):
        copy.wait()
        for k in range(q * span, (q + 1) * span, piece):
            kept = jnp.transpose(kept_ref[:, k : k + piece])
            taken = jnp.transpose(taken_ref[:, k : k + piece])

            @pl.when(core == 0)
            def _():
                out_ref[k : k + piece, :rows] = kept
                out_ref[k : k + piece, rows:] = taken

            @pl.when(core != 0)
            def _():
                out_ref[k : k + piece, :rows] = taken
                out_ref[k : k + piece, rows:] = kept


def fold_kernel(turn, blocks, inverse_ref, *refs):
    base_refs = refs[:blocks]
    in_refs = refs[blocks : 2 * blocks] if turn else ()
    out_ref = refs[-1]
    wave_rows, rows = out_ref.shape
    forward, _, wave, fed = own_turn(turn)
    chip = own_place()[0]
    here = pl.ds(pl.multiple_of(wave * wave_rows, wave_rows), wave_rows)
    total = jnp.zeros((wave_rows, rows), F32)
    for i in range(blocks):
        if turn:
            base = jnp.where(forward, base_refs[i][here, :].astype(F32), 0.0)
            vectors = (jnp.where(fed, in_refs[i][...].astype(F32), 0.0) + base).astype(BF16)
        else:
            vectors = base_refs[i][here, :]
        place = pl.ds(pl.multiple_of(((chip // 2) ^ i) * rows, rows), rows)
        total += jnp.dot(vectors, inverse_ref[place, :], preferred_element_type=F32)
    out_ref[...] = total.astype(BF16)


def join_kernel(turn, mine_ref, other_ref, state_ref, scale_ref, next_ref, out_ref):
    wave_rows = mine_ref.shape[0]
    forward, backward, wave, _ = own_turn(turn)
    here = pl.ds(pl.multiple_of(wave * wave_rows, wave_rows), wave_rows)
    solved = (mine_ref[...].astype(F32) + other_ref[...].astype(F32)).astype(BF16).astype(F32)
    older = state_ref[here, :].astype(F32)
    field = (solved + jnp.where(backward, older, 0.0)).astype(BF16)
    scale = jnp.where(backward, scale_ref[1:2, :], scale_ref[0:1, :])
    out_ref[...] = (scale * field.astype(F32)).astype(BF16)

    @pl.when(forward | backward)
    def _():
        next_ref[here, :] = field


def turn_routes(turn, panels, waves):
    at = [s if s < panels else 2 * (panels - 1) - s for s in range(2 * panels - 1)]
    pairs = []
    for wave in range(waves):
        step = turn - wave
        if 0 <= step < 2 * (panels - 1):
            pairs.append((at[step], at[step + 1]))
    sources = [a for a, _ in pairs]
    targets = [b for _, b in pairs]
    for panel in range(panels):
        if panel not in sources and panel not in targets:
            pairs.append((panel, panel))
    spare = [p for p in targets if p not in sources]
    unfed = [p for p in sources if p not in targets]
    return pairs + list(zip(spare, unfed))


def spread(values, panel_pairs, chips):
    received = []
    for i in range(chips // 2):
        route = []
        for start, end in panel_pairs:
            for chip in range(chips):
                for core in range(2):
                    there = chip ^ (2 * i + core)
                    route.append(
                        (2 * (start * chips + chip) + core, 2 * (end * chips + there) + core)
                    )
        received.append(lax.ppermute(values, ("panel", "front"), route))
    return received


def body(top_source, leaf_source, top_inverse, leaf_inverse, boundary, touch_rows, coupling):
    sources = top_source.shape[1]
    rows = top_source.shape[2]
    width = top_inverse.shape[2]
    leaf_count, leaf_size = leaf_inverse.shape[1:3]
    edge = boundary.shape[2]
    panels = lax.axis_size("panel")
    front = lax.axis_size("front")
    chips, half = front // 2, front // 4
    chip_rows = 2 * rows
    panel = lax.axis_index("panel")
    core = lax.axis_index("front") % 2
    wave_rows = sources // WAVES
    group = group_of(leaf_count, 6)
    steps = leaf_count // group
    all_lanes = leaf_count * leaf_size

    swap_core = [(i, i ^ 1) for i in range(front)]
    swap_chip = [(i, i + 1) for i in range(1, front - 1, 2)]
    swap_chip = swap_chip + [(j, i) for i, j in swap_chip]

    outward, partial, interior = pl.pallas_call(
        functools.partial(push_kernel, group),
        out_shape=(
            pltpu.VMEM((sources, rows), BF16),
            pltpu.VMEM((sources, chip_rows), F32),
            pltpu.VMEM((sources, all_lanes), BF16),
        ),
        in_specs=[VMEM, VMEM, ANY, ANY, ANY],
        out_specs=(VMEM, VMEM, VMEM),
        scratch_shapes=[
            pltpu.VMEM((sources, all_lanes), BF16),
            pltpu.VMEM((leaf_count, leaf_size, leaf_size), BF16),
            pltpu.VMEM((leaf_count, edge, leaf_size), BF16),
            pltpu.VMEM((2, group * edge, 3 * rows), BF16),
            pltpu.VMEM((sources, 3 * rows), F32),
            pltpu.SemaphoreType.DMA((steps, 3)),
        ],
        compiler_params=params(20),
    )(
        touch_rows[0],
        top_source[0],
        in_hbm(leaf_source[0]),
        in_hbm(leaf_inverse[0]),
        in_hbm(boundary[0]),
    )
    inward = lax.ppermute(outward, "front", swap_chip)
    blank = jnp.zeros_like(partial[:, :rows])
    whole_inward = jnp.where(
        core == 0,
        jnp.concatenate([inward.astype(F32), blank], axis=1),
        jnp.concatenate([blank, inward.astype(F32)], axis=1),
    )
    partial = (partial - whole_inward).astype(BF16)
    partner = lax.ppermute(partial, "front", swap_core)
    known = (partial.astype(F32) + partner.astype(F32)).astype(BF16)
    base = [in_vmem(b) for b in spread(known, [(p, p) for p in range(panels)], chips)]

    given = pl.pallas_call(
        half_kernel,
        out_shape=jax.ShapeDtypeStruct((rows, width // 2), BF16),
        in_specs=[ANY, ANY],
        out_specs=VMEM,
        scratch_shapes=[pltpu.SemaphoreType.DMA((half,))],
        compiler_params=params(4),
    )(in_hbm(top_inverse[0]), outward)
    taken = lax.ppermute(given, "front", swap_core)
    inverse = pl.pallas_call(
        turn_kernel,
        out_shape=pltpu.VMEM((width // 2, chip_rows), BF16),
        in_specs=[ANY, VMEM],
        out_specs=VMEM,
        scratch_shapes=[
            pltpu.VMEM((rows, width // 2), BF16),
            pltpu.SemaphoreType.DMA((half,)),
        ],
        compiler_params=params(8),
    )(in_hbm(top_inverse[0]), taken)
    inverse = in_vmem(inverse)

    coupling, _ = lax.optimization_barrier((coupling, outward))
    later = lax.ppermute(coupling, "panel", [((p + 1) % panels, p) for p in range(panels)])
    forward_scale = jnp.where(panel == panels - 1, coupling, later)
    scales = jnp.concatenate([forward_scale, coupling], axis=0)
    partner_scales = lax.ppermute(scales, "front", swap_core)
    scales = jnp.where(
        core == 0,
        jnp.concatenate([scales, partner_scales], axis=1),
        jnp.concatenate([partner_scales, scales], axis=1),
    )
    scales = in_vmem(scales)
    state = jnp.zeros((sources, chip_rows), BF16)
    turns = 2 * (panels - 1) + WAVES
    arrived, extra = [], []
    for turn in range(turns):
        share = pl.pallas_call(
            functools.partial(fold_kernel, turn, half),
            out_shape=pltpu.VMEM((wave_rows, chip_rows), BF16),
            in_specs=[VMEM] * (1 + half + len(arrived)) + [ANY] * len(extra),
            out_specs=VMEM,
            compiler_params=params(4),
        )(inverse, *base, *arrived, *extra)
        extra = []
        other = lax.ppermute(share, "front", swap_core)
        state, outgoing = pl.pallas_call(
            functools.partial(join_kernel, turn),
            out_shape=(
                pltpu.VMEM((sources, chip_rows), BF16),
                pltpu.VMEM((wave_rows, chip_rows), BF16),
            ),
            in_specs=[VMEM] * 4,
            out_specs=(VMEM, VMEM),
            input_output_aliases={2: 0},
            compiler_params=params(4),
        )(in_vmem(share), in_vmem(other), in_vmem(state), scales)
        if turn < turns - 1:
            routes = turn_routes(turn, panels, WAVES)
            arrived = [in_vmem(a) for a in spread(outgoing, routes, chips)]
        if turn == 1:
            picks = pl.pallas_call(
                pick_kernel,
                out_shape=pltpu.VMEM((3 * rows, leaf_count * edge), BF16),
                in_specs=[VMEM, ANY],
                out_specs=VMEM,
                compiler_params=params(4),
                cost_estimate=pl.CostEstimate(
                    flops=4 * sources * rows * leaf_count * edge,
                    bytes_accessed=6 * rows * leaf_count * edge,
                    transcendentals=0,
                ),
            )(touch_rows[0], outgoing)
            extra = [in_vmem(picks)]
        if turn == 2:
            matrices = pl.pallas_call(
                functools.partial(lift_matrix_kernel, group),
                out_shape=pltpu.VMEM((leaf_count, edge, leaf_size), BF16),
                in_specs=[ANY, ANY, ANY],
                out_specs=VMEM,
                scratch_shapes=[
                    pltpu.VMEM((leaf_count, leaf_size, leaf_size), BF16),
                    pltpu.VMEM((leaf_count, edge, leaf_size), BF16),
                    pltpu.SemaphoreType.DMA((steps, 2)),
                ],
                compiler_params=params(12),
                cost_estimate=pl.CostEstimate(
                    flops=2 * leaf_count * edge * leaf_size * leaf_size,
                    bytes_accessed=4 * leaf_count * leaf_size * leaf_size,
                    transcendentals=0,
                ),
            )(in_hbm(leaf_inverse[0]), in_hbm(boundary[0]), outgoing)
            extra = [in_vmem(matrices)]

    top_field = jnp.where(core == 0, state[:, :rows], state[:, rows:])
    beside = lax.ppermute(top_field, "front", swap_chip)
    picked = pl.pallas_call(
        near_kernel,
        out_shape=pltpu.VMEM((sources, leaf_count * edge), BF16),
        in_specs=[VMEM] * 2,
        out_specs=VMEM,
        compiler_params=params(8),
        cost_estimate=pl.CostEstimate(
            flops=4 * sources * rows * leaf_count * edge,
            bytes_accessed=4 * rows * leaf_count * edge,
            transcendentals=0,
        ),
    )(in_vmem(state), in_vmem(picks))
    leaf_field = pl.pallas_call(
        functools.partial(leaf_kernel, group),
        out_shape=jax.ShapeDtypeStruct((sources, all_lanes), BF16),
        in_specs=[VMEM] * 5,
        out_specs=ANY,
        scratch_shapes=[
            pltpu.VMEM((sources, all_lanes), BF16),
            pltpu.SemaphoreType.DMA((steps,)),
        ],
        compiler_params=params(8),
    )(in_vmem(beside), in_vmem(picked), in_vmem(picks), in_vmem(matrices), in_vmem(interior))
    return (top_field[None], leaf_field[None])


def solution(mesh):
    placed = (
        P("panel", None, "front"),
        P("panel", None, "front"),
        P("panel", "front", None),
        P("panel", "front", None, None),
        P("panel", "front", None, None),
        P("panel", "front", None),
        P("panel", "front"),
    )
    return jax.shard_map(
        body,
        mesh=mesh,
        in_specs=placed,
        out_specs=(P("panel", None, "front"), P("panel", None, "front")),
        check_vma=False,
    )
```

```python
import functools

import jax
import jax.numpy as jnp
from jax import lax
from jax.experimental import pallas as pl
from jax.experimental.pallas import tpu as pltpu
from jax.sharding import PartitionSpec as P

WAVES = 2
F32 = jnp.float32
BF16 = jnp.bfloat16
VMEM = pl.BlockSpec(memory_space=pltpu.VMEM)
ANY = pl.BlockSpec(memory_space=pl.ANY)


def params(mib):
    return pltpu.CompilerParams(vmem_limit_bytes=mib * 1024 * 1024)


def in_vmem(value):
    return pltpu.with_memory_space_constraint(value, pltpu.VMEM)


def in_hbm(value):
    return pltpu.with_memory_space_constraint(value, pltpu.HBM)


def rows_dot(left, right):
    return lax.dot_general(left, right, (((1,), (1,)), ((), ())), preferred_element_type=F32)


def group_of(leaf_count, most):
    return max(g for g in range(1, most + 1) if leaf_count % g == 0)


def own_place():
    place = lax.axis_index("front")
    return place // 2, place % 2


def own_turn(turn):
    panel = lax.axis_index("panel")
    panels = lax.axis_size("panel")
    up_wave = turn - panel
    down_wave = turn - (2 * (panels - 1) - panel)
    up = (up_wave >= 0) & (up_wave < WAVES)
    down = (down_wave >= 0) & (down_wave < WAVES) & (panel < panels - 1)
    wave = jnp.where(up, up_wave, jnp.where(down, down_wave, 0))
    return up, down, wave


def push_kernel(
    group,
    rows_ref,
    top_ref,
    source_hbm,
    inverse_hbm,
    boundary_hbm,
    solver_hbm,
    outward_ref,
    partial_ref,
    interior_ref,
    given_ref,
    source_ref,
    inverse_ref,
    boundary_ref,
    pick_ref,
    total_ref,
    half_sems,
    sems,
):
    leaf_count, leaf_size = inverse_ref.shape[:2]
    edge = boundary_ref.shape[1]
    rows = top_ref.shape[2]
    window = 3 * rows
    chip, core = own_place()
    copies = []
    for step in range(leaf_count // group):
        leaves = pl.ds(step * group, group)
        lanes = pl.ds(step * group * leaf_size, group * leaf_size)
        parts = (
            (source_hbm.at[:, lanes], source_ref.at[:, lanes]),
            (inverse_hbm.at[leaves], inverse_ref.at[leaves]),
            (boundary_hbm.at[leaves], boundary_ref.at[leaves]),
        )
        copies.append(
            [pltpu.make_async_copy(a, b, sems.at[step, i]) for i, (a, b) in enumerate(parts)]
        )
        for copy in copies[-1]:
            copy.start()
    staged = sum(half_copies((chip + core + 1) % 2, solver_hbm, given_ref, half_sems), [])
    places = lax.broadcasted_iota(jnp.int16, (edge, window), 1)
    for step in range(leaf_count // group):
        for copy in copies[step]:
            copy.wait()
        first = step * group
        interior = []
        for j in range(first, first + group):
            lanes = slice(j * leaf_size, (j + 1) * leaf_size)
            interior.append(rows_dot(source_ref[:, lanes], inverse_ref[j]).astype(BF16))
            interior_ref[:, lanes] = interior[-1]
        pushed = [
            rows_dot(interior[g], boundary_ref[first + g]).astype(BF16) for g in range(group)
        ]
        if step == 0:
            lines = [rows_ref[i] for i in range(rows_ref.shape[0])]
            if leaf_count % 8:
                lines.append(jnp.zeros((-leaf_count % 8, edge), jnp.int32))
            local = jnp.concatenate(lines, axis=0) - (lax.axis_index("front") - 1) * rows
            columns = jnp.transpose(local).astype(jnp.int16)
        for g in range(group):
            pick_ref[step % 2, g * edge : (g + 1) * edge, :] = jnp.where(
                columns[:, first + g : first + g + 1] == places, jnp.bfloat16(1), jnp.bfloat16(0)
            )
        total = jnp.dot(
            jnp.concatenate(pushed, axis=1), pick_ref[step % 2], preferred_element_type=F32
        )
        if step == 0:
            total_ref[...] = total
        else:
            total_ref[...] += total
    for copy in staged:
        copy.wait()
    top = top_ref[0].astype(F32)

    @pl.when(core == 0)
    def _():
        outward_ref[...] = total_ref[:, :rows].astype(BF16)
        partial_ref[:, :rows] = top - total_ref[:, rows : 2 * rows]
        partial_ref[:, rows:] = -total_ref[:, 2 * rows :]

    @pl.when(core != 0)
    def _():
        outward_ref[...] = total_ref[:, 2 * rows :].astype(BF16)
        partial_ref[:, :rows] = -total_ref[:, :rows]
        partial_ref[:, rows:] = top - total_ref[:, rows : 2 * rows]


def pick_kernel(rows_ref, after_ref, out_ref):
    tile, edge = rows_ref.shape[1:]
    leaf_count = rows_ref.shape[0] * tile
    window = out_ref.shape[0]
    rows = window // 3
    place = lax.axis_index("front")
    local = rows_ref[...] - (place - 1) * rows
    shifted = jnp.where(local < rows, local + 2 * rows, local - rows)
    local = jnp.where(place % 2 == 0, shifted, local)
    places = lax.broadcasted_iota(jnp.int16, (window, edge), 0)
    for j in range(leaf_count):
        out_ref[:, j * edge : (j + 1) * edge] = jnp.where(
            local[j // tile, j % tile : j % tile + 1, :].astype(jnp.int16) == places,
            jnp.bfloat16(1),
            jnp.bfloat16(0),
        )


def lift_matrix_kernel(group, inverse_hbm, boundary_hbm, after_ref, out_ref, inverse_ref, boundary_ref, sems):
    leaf_count = out_ref.shape[0]
    copies = []
    for step in range(leaf_count // group):
        leaves = pl.ds(step * group, group)
        parts = (
            (inverse_hbm.at[leaves], inverse_ref.at[leaves]),
            (boundary_hbm.at[leaves], boundary_ref.at[leaves]),
        )
        copies.append(
            [pltpu.make_async_copy(a, b, sems.at[step, i]) for i, (a, b) in enumerate(parts)]
        )
        for copy in copies[-1]:
            copy.start()
    for step in range(leaf_count // group):
        for copy in copies[step]:
            copy.wait()
        for j in range(step * group, (step + 1) * group):
            out_ref[j] = rows_dot(boundary_ref[j], inverse_ref[j]).astype(BF16)


def near_kernel(state_ref, pick_ref, out_ref):
    out_ref[...] = jnp.dot(
        state_ref[...], pick_ref[: state_ref.shape[1], :], preferred_element_type=F32
    ).astype(BF16)


def leaf_kernel(
    group,
    beside_ref,
    picked_ref,
    pick_ref,
    matrix_ref,
    interior_ref,
    top_ref,
    out_hbm,
    top_hbm,
    out_ref,
    top_sem,
    sems,
):
    leaf_count, edge, leaf_size = matrix_ref.shape
    rows = beside_ref.shape[1]
    beside = beside_ref[...]
    copies = [pltpu.make_async_copy(top_ref, top_hbm, top_sem)]
    copies[0].start()
    for step in range(leaf_count // group):
        first = step * group
        span = slice(first * edge, (first + group) * edge)
        picked = jnp.dot(beside, pick_ref[2 * rows :, span], preferred_element_type=F32)
        picked = (picked + picked_ref[:, span].astype(F32)).astype(BF16)
        for g in range(group):
            lanes = slice((first + g) * leaf_size, (first + g + 1) * leaf_size)
            lifted = jnp.dot(
                picked[:, g * edge : (g + 1) * edge],
                matrix_ref[first + g],
                preferred_element_type=F32,
            )
            out_ref[:, lanes] = (interior_ref[:, lanes].astype(F32) - lifted).astype(BF16)
        lanes = pl.ds(first * leaf_size, group * leaf_size)
        copies.append(
            pltpu.make_async_copy(out_ref.at[:, lanes], out_hbm.at[:, lanes], sems.at[step])
        )
        copies[-1].start()
    for copy in copies:
        copy.wait()


def half_copies(parity, inverse_hbm, to_ref, sems):
    pairs, pieces = sems.shape
    span = to_ref.shape[1] // pairs
    tall = to_ref.shape[0] // pieces
    copies = []
    for q in range(pairs):
        start = pl.multiple_of((2 * q + parity) * span, span)
        copies.append([])
        for r in range(pieces):
            here = pl.ds(r * tall, tall)
            copies[-1].append(
                pltpu.make_async_copy(
                    inverse_hbm.at[here, pl.ds(start, span)],
                    to_ref.at[here, pl.ds(q * span, span)],
                    sems.at[q, r],
                )
            )
            copies[-1][-1].start()
    return copies


def turn_kernel(inverse_hbm, taken_hbm, out_ref, kept_ref, taken_ref, kept_sems, taken_sems):
    chip, core = own_place()
    rows = taken_ref.shape[0]
    span = kept_ref.shape[1] // kept_sems.shape[0]
    taken_copies = []
    for q in range(taken_sems.shape[0]):
        lanes = pl.ds(q * span, span)
        taken_copies.append(
            pltpu.make_async_copy(taken_hbm.at[:, lanes], taken_ref.at[:, lanes], taken_sems.at[q])
        )
        taken_copies[-1].start()
    kept_copies = half_copies((chip + core) % 2, inverse_hbm, kept_ref, kept_sems)
    piece = min(span, 256)
    for q in range(len(kept_copies)):
        taken_copies[q].wait()
        for copy in kept_copies[q]:
            copy.wait()
        for k in range(q * span, (q + 1) * span, piece):
            kept = jnp.transpose(kept_ref[:, k : k + piece])
            taken = jnp.transpose(taken_ref[:, k : k + piece])

            @pl.when(core == 0)
            def _():
                out_ref[k : k + piece, :rows] = kept
                out_ref[k : k + piece, rows:] = taken

            @pl.when(core != 0)
            def _():
                out_ref[k : k + piece, :rows] = taken
                out_ref[k : k + piece, rows:] = kept


def fold_kernel(blocks, more, skipped, inverse_ref, *refs):
    refs = refs[skipped:]
    out_ref = refs[-1]
    wave_rows, rows = out_ref.shape
    chip = own_place()[0]
    total = refs[-2][...] if more else jnp.zeros((wave_rows, rows), F32)
    for n, i in enumerate(blocks):
        place = pl.ds(pl.multiple_of(((chip // 2) ^ i) * rows, rows), rows)
        total += jnp.dot(refs[n][...], inverse_ref[place, :], preferred_element_type=F32)
    out_ref[...] = total.astype(out_ref.dtype)


def join_kernel(
    turn, mine_ref, other_ref, state_ref, scale_ref, later_ref, next_ref, out_ref
):
    wave_rows = mine_ref.shape[0]
    last = lax.axis_index("panel") == lax.axis_size("panel") - 1
    forward, backward, wave = own_turn(turn)
    here = pl.ds(pl.multiple_of(wave * wave_rows, wave_rows), wave_rows)
    solved = (mine_ref[...].astype(F32) + other_ref[...].astype(F32)).astype(BF16).astype(F32)
    older = state_ref[here, :].astype(F32)
    field = (solved + jnp.where(backward, older, 0.0)).astype(BF16)
    scale = jnp.where(backward, scale_ref[1:2, :], scale_ref[0:1, :])
    ahead = jnp.where(forward & ~last, later_ref[here, :].astype(F32), 0.0)
    out_ref[...] = (scale * field.astype(F32) + ahead).astype(BF16)
    if turn == 0:

        @pl.when(last)
        def _():
            out_ref[...] = later_ref[wave_rows : 2 * wave_rows, :]

    @pl.when(forward | backward)
    def _():
        next_ref[here, :] = field


def turn_routes(turn, panels, waves):
    if turn == 0:
        return [(p, (p + 1) % panels) for p in range(panels)]
    at = [s if s < panels else 2 * (panels - 1) - s for s in range(2 * panels - 1)]
    pairs = []
    for wave in range(waves):
        step = turn - wave
        if 0 <= step < 2 * (panels - 1):
            pairs.append((at[step], at[step + 1]))
    sources = [a for a, _ in pairs]
    targets = [b for _, b in pairs]
    for panel in range(panels):
        if panel not in sources and panel not in targets:
            pairs.append((panel, panel))
    spare = [p for p in targets if p not in sources]
    unfed = [p for p in sources if p not in targets]
    return pairs + list(zip(spare, unfed))


def spread(values, panel_pairs, chips):
    received = []
    for i in range(chips // 2):
        route = []
        for start, end in panel_pairs:
            for chip in range(chips):
                for core in range(2):
                    there = chip ^ (2 * i + core)
                    route.append(
                        (2 * (start * chips + chip) + core, 2 * (end * chips + there) + core)
                    )
        received.append(lax.ppermute(values, ("panel", "front"), route))
    return received


def body(top_source, leaf_source, top_inverse, leaf_inverse, boundary, touch_rows, coupling):
    sources = top_source.shape[1]
    rows = top_source.shape[2]
    width = top_inverse.shape[2]
    leaf_count, leaf_size = leaf_inverse.shape[1:3]
    edge = boundary.shape[2]
    panels = lax.axis_size("panel")
    front = lax.axis_size("front")
    chips, half = front // 2, front // 4
    chip_rows = 2 * rows
    panel = lax.axis_index("panel")
    core = lax.axis_index("front") % 2
    wave_rows = sources // WAVES
    group = group_of(leaf_count, 6)
    steps = leaf_count // group
    all_lanes = leaf_count * leaf_size

    swap_core = [(i, i ^ 1) for i in range(front)]
    swap_chip = [(i, i + 1) for i in range(1, front - 1, 2)]
    swap_chip = swap_chip + [(j, i) for i, j in swap_chip]

    tile = group_of(leaf_count, 8 if leaf_count % 8 == 0 else 4)
    touch_rows = touch_rows.reshape(leaf_count // tile, tile, edge)
    pieces = group_of(rows // 16, 8)
    outward, partial, interior, given = pl.pallas_call(
        functools.partial(push_kernel, group),
        out_shape=(
            pltpu.VMEM((sources, rows), BF16),
            pltpu.VMEM((sources, chip_rows), F32),
            pltpu.VMEM((sources, all_lanes), BF16),
            pltpu.VMEM((rows, width // 2), BF16),
        ),
        in_specs=[VMEM] * 2 + [ANY] * 4,
        out_specs=(VMEM, VMEM, VMEM, VMEM),
        scratch_shapes=[
            pltpu.VMEM((sources, all_lanes), BF16),
            pltpu.VMEM((leaf_count, leaf_size, leaf_size), BF16),
            pltpu.VMEM((leaf_count, edge, leaf_size), BF16),
            pltpu.VMEM((2, group * edge, 3 * rows), BF16),
            pltpu.VMEM((sources, 3 * rows), F32),
            pltpu.SemaphoreType.DMA((half, pieces)),
            pltpu.SemaphoreType.DMA((steps, 3)),
        ],
        compiler_params=params(24),
    )(
        touch_rows,
        top_source,
        in_hbm(leaf_source[0]),
        in_hbm(leaf_inverse[0]),
        in_hbm(boundary[0]),
        in_hbm(top_inverse[0]),
    )
    coupling, given, outward = lax.optimization_barrier((coupling, given, outward))
    taken = lax.ppermute(given, "front", swap_core)
    inward = lax.ppermute(outward, "front", swap_chip)
    ring = [((p + 1) % panels, p) for p in range(panels)]
    later = lax.ppermute(coupling, "panel", ring)
    inward, later = lax.optimization_barrier((inward, later))
    forward_scale = jnp.where(panel == panels - 1, coupling, later)
    scales = jnp.concatenate([forward_scale, coupling], axis=0)
    blank = jnp.zeros_like(partial[:, :rows])
    whole_inward = jnp.where(
        core == 0,
        jnp.concatenate([inward.astype(F32), blank], axis=1),
        jnp.concatenate([blank, inward.astype(F32)], axis=1),
    )
    partial = (partial - whole_inward).astype(BF16)
    partner = lax.ppermute(partial, "front", swap_core)
    partner_scales = lax.ppermute(scales, "front", swap_core)
    known = (partial.astype(F32) + partner.astype(F32)).astype(BF16)
    scales = jnp.where(
        core == 0,
        jnp.concatenate([scales, partner_scales], axis=1),
        jnp.concatenate([partner_scales, scales], axis=1),
    )
    scales = in_vmem(scales)
    arrived = [in_vmem(a) for a in spread(known[:wave_rows], [(0, 0)], chips)]
    later_known = in_vmem(lax.ppermute(known, "panel", ring))

    inverse = pl.pallas_call(
        turn_kernel,
        out_shape=pltpu.VMEM((width // 2, chip_rows), BF16),
        in_specs=[ANY, ANY],
        out_specs=VMEM,
        scratch_shapes=[
            pltpu.VMEM((rows, width // 2), BF16),
            pltpu.VMEM((rows, width // 2), BF16),
            pltpu.SemaphoreType.DMA((half, pieces)),
            pltpu.SemaphoreType.DMA((half,)),
        ],
        compiler_params=params(8),
        cost_estimate=pl.CostEstimate(
            flops=2 * sources * width * rows, bytes_accessed=4 * width * rows, transcendentals=0
        ),
    )(in_hbm(top_inverse[0]), taken)
    inverse = in_vmem(inverse)

    state = jnp.zeros((sources, chip_rows), BF16)
    turns = 2 * (panels - 1) + WAVES
    extra = []
    for turn in range(turns):
        share = ()
        halves = (range(half // 2, half), range(half // 2)) if turn else (range(half),)
        for blocks in halves:
            last = blocks is halves[-1]
            behind = extra if last else []
            operands = [arrived[i] for i in blocks] + [in_vmem(v) for v in share]
            share = (
                pl.pallas_call(
                    functools.partial(fold_kernel, blocks, bool(share), len(behind)),
                    out_shape=pltpu.VMEM((wave_rows, chip_rows), BF16 if last else F32),
                    in_specs=[VMEM] + [ANY] * len(behind) + [VMEM] * len(operands),
                    out_specs=VMEM,
                    compiler_params=params(4),
                )(inverse, *behind, *operands),
            )
        share, extra = share[0], []
        other = lax.ppermute(share, "front", swap_core)
        state, outgoing = pl.pallas_call(
            functools.partial(join_kernel, turn),
            out_shape=(
                pltpu.VMEM((sources, chip_rows), BF16),
                pltpu.VMEM((wave_rows, chip_rows), BF16),
            ),
            in_specs=[VMEM] * 5,
            out_specs=(VMEM, VMEM),
            input_output_aliases={2: 0},
            compiler_params=params(4),
        )(in_vmem(share), in_vmem(other), in_vmem(state), scales, later_known)
        if turn < turns - 1:
            routes = turn_routes(turn, panels, WAVES)
            arrived = [in_vmem(a) for a in spread(outgoing, routes, chips)]
        if turn == 1:
            picks = pl.pallas_call(
                pick_kernel,
                out_shape=pltpu.VMEM((3 * rows, leaf_count * edge), BF16),
                in_specs=[VMEM, ANY],
                out_specs=VMEM,
                compiler_params=params(4),
                cost_estimate=pl.CostEstimate(
                    flops=4 * sources * rows * leaf_count * edge,
                    bytes_accessed=6 * rows * leaf_count * edge,
                    transcendentals=0,
                ),
            )(touch_rows, outgoing)
            extra = [in_vmem(picks)]
        if turn == 2:
            matrices = pl.pallas_call(
                functools.partial(lift_matrix_kernel, group),
                out_shape=pltpu.VMEM((leaf_count, edge, leaf_size), BF16),
                in_specs=[ANY, ANY, ANY],
                out_specs=VMEM,
                scratch_shapes=[
                    pltpu.VMEM((leaf_count, leaf_size, leaf_size), BF16),
                    pltpu.VMEM((leaf_count, edge, leaf_size), BF16),
                    pltpu.SemaphoreType.DMA((steps, 2)),
                ],
                compiler_params=params(12),
                cost_estimate=pl.CostEstimate(
                    flops=2 * leaf_count * edge * leaf_size * leaf_size,
                    bytes_accessed=4 * leaf_count * leaf_size * leaf_size,
                    transcendentals=0,
                ),
            )(in_hbm(leaf_inverse[0]), in_hbm(boundary[0]), outgoing)
            extra = [in_vmem(matrices)]

    top_field = jnp.where(core == 0, state[:, :rows], state[:, rows:])
    beside = lax.ppermute(top_field, "front", swap_chip)
    picked = pl.pallas_call(
        near_kernel,
        out_shape=pltpu.VMEM((sources, leaf_count * edge), BF16),
        in_specs=[VMEM] * 2,
        out_specs=VMEM,
        compiler_params=params(8),
        cost_estimate=pl.CostEstimate(
            flops=4 * sources * rows * leaf_count * edge,
            bytes_accessed=4 * rows * leaf_count * edge,
            transcendentals=0,
        ),
    )(in_vmem(state), in_vmem(picks))
    leaf_field, top_field = pl.pallas_call(
        functools.partial(leaf_kernel, group),
        out_shape=(
            jax.ShapeDtypeStruct((sources, all_lanes), BF16),
            jax.ShapeDtypeStruct((sources, rows), BF16),
        ),
        in_specs=[VMEM] * 6,
        out_specs=(ANY, ANY),
        scratch_shapes=[
            pltpu.VMEM((sources, all_lanes), BF16),
            pltpu.SemaphoreType.DMA,
            pltpu.SemaphoreType.DMA((steps,)),
        ],
        compiler_params=params(8),
    )(in_vmem(beside), in_vmem(picked), in_vmem(picks), in_vmem(matrices), in_vmem(interior), in_vmem(top_field))
    return (top_field[None], leaf_field[None])


def solution(mesh):
    placed = (
        P("panel", None, "front"),
        P("panel", None, "front"),
        P("panel", "front", None),
        P("panel", "front", None, None),
        P("panel", "front", None, None),
        P("panel", "front", None),
        P("panel", "front"),
    )
    return jax.shard_map(
        body,
        mesh=mesh,
        in_specs=placed,
        out_specs=(P("panel", None, "front"), P("panel", None, "front")),
        check_vma=False,
    )
```

```python
import functools

import jax
import jax.numpy as jnp
from jax import lax
from jax.experimental import pallas as pl
from jax.experimental.pallas import tpu as pltpu
from jax.sharding import PartitionSpec as P

WAVES = 2
F32 = jnp.float32
BF16 = jnp.bfloat16
VMEM = pl.BlockSpec(memory_space=pltpu.VMEM)
ANY = pl.BlockSpec(memory_space=pl.ANY)


def params(mib):
    return pltpu.CompilerParams(vmem_limit_bytes=mib * 1024 * 1024)


def in_vmem(value):
    return pltpu.with_memory_space_constraint(value, pltpu.VMEM)


def in_hbm(value):
    return pltpu.with_memory_space_constraint(value, pltpu.HBM)


def rows_dot(left, right):
    return lax.dot_general(left, right, (((1,), (1,)), ((), ())), preferred_element_type=F32)


def group_of(leaf_count, most):
    return max(g for g in range(1, most + 1) if leaf_count % g == 0)


def own_place():
    place = lax.axis_index("front")
    return place // 2, place % 2


def own_half():
    chip, core = own_place()
    return (chip // (lax.axis_size("front") // 4)) ^ core


def own_turn(turn):
    panel = lax.axis_index("panel")
    panels = lax.axis_size("panel")
    up_wave = turn - panel
    down_wave = turn - (2 * (panels - 1) - panel)
    up = (up_wave >= 0) & (up_wave < WAVES)
    down = (down_wave >= 0) & (down_wave < WAVES) & (panel < panels - 1)
    wave = jnp.where(up, up_wave, jnp.where(down, down_wave, 0))
    return up, down, wave


def push_kernel(
    group,
    rows_ref,
    top_ref,
    source_hbm,
    inverse_hbm,
    boundary_hbm,
    solver_hbm,
    outward_ref,
    partial_ref,
    interior_ref,
    given_ref,
    source_ref,
    inverse_ref,
    boundary_ref,
    pick_ref,
    total_ref,
    half_sems,
    sems,
):
    leaf_count, leaf_size = inverse_ref.shape[:2]
    edge = boundary_ref.shape[1]
    rows = top_ref.shape[2]
    window = 3 * rows
    core = own_place()[1]
    copies = []
    for step in range(leaf_count // group):
        leaves = pl.ds(step * group, group)
        lanes = pl.ds(step * group * leaf_size, group * leaf_size)
        parts = (
            (source_hbm.at[:, lanes], source_ref.at[:, lanes]),
            (inverse_hbm.at[leaves], inverse_ref.at[leaves]),
            (boundary_hbm.at[leaves], boundary_ref.at[leaves]),
        )
        copies.append(
            [pltpu.make_async_copy(a, b, sems.at[step, i]) for i, (a, b) in enumerate(parts)]
        )
        for copy in copies[-1]:
            copy.start()
    staged = sum(half_copies(1 - own_half(), solver_hbm, given_ref, half_sems), [])
    places = lax.broadcasted_iota(jnp.int16, (edge, window), 1)
    for step in range(leaf_count // group):
        for copy in copies[step]:
            copy.wait()
        first = step * group
        interior = []
        for j in range(first, first + group):
            lanes = slice(j * leaf_size, (j + 1) * leaf_size)
            interior.append(rows_dot(source_ref[:, lanes], inverse_ref[j]).astype(BF16))
            interior_ref[:, lanes] = interior[-1]
        pushed = [
            rows_dot(interior[g], boundary_ref[first + g]).astype(BF16) for g in range(group)
        ]
        if step == 0:
            lines = [rows_ref[i] for i in range(rows_ref.shape[0])]
            if leaf_count % 8:
                lines.append(jnp.zeros((-leaf_count % 8, edge), jnp.int32))
            local = jnp.concatenate(lines, axis=0) - (lax.axis_index("front") - 1) * rows
            columns = jnp.transpose(local).astype(jnp.int16)
        for g in range(group):
            pick_ref[step % 2, g * edge : (g + 1) * edge, :] = jnp.where(
                columns[:, first + g : first + g + 1] == places, jnp.bfloat16(1), jnp.bfloat16(0)
            )
        total = jnp.dot(
            jnp.concatenate(pushed, axis=1), pick_ref[step % 2], preferred_element_type=F32
        )
        if step == 0:
            total_ref[...] = total
        else:
            total_ref[...] += total
    for copy in staged:
        copy.wait()
    top = top_ref[0].astype(F32)

    @pl.when(core == 0)
    def _():
        outward_ref[...] = total_ref[:, :rows].astype(BF16)
        partial_ref[:, :rows] = top - total_ref[:, rows : 2 * rows]
        partial_ref[:, rows:] = -total_ref[:, 2 * rows :]

    @pl.when(core != 0)
    def _():
        outward_ref[...] = total_ref[:, 2 * rows :].astype(BF16)
        partial_ref[:, :rows] = -total_ref[:, :rows]
        partial_ref[:, rows:] = top - total_ref[:, rows : 2 * rows]


def pick_kernel(rows_ref, after_ref, out_ref):
    tile, edge = rows_ref.shape[1:]
    leaf_count = rows_ref.shape[0] * tile
    window = out_ref.shape[0]
    rows = window // 3
    place = lax.axis_index("front")
    local = rows_ref[...] - (place - 1) * rows
    shifted = jnp.where(local < rows, local + 2 * rows, local - rows)
    local = jnp.where(place % 2 == 0, shifted, local)
    places = lax.broadcasted_iota(jnp.int16, (window, edge), 0)
    for j in range(leaf_count):
        out_ref[:, j * edge : (j + 1) * edge] = jnp.where(
            local[j // tile, j % tile : j % tile + 1, :].astype(jnp.int16) == places,
            jnp.bfloat16(1),
            jnp.bfloat16(0),
        )


def lift_matrix_kernel(group, inverse_hbm, boundary_hbm, after_ref, out_ref, inverse_ref, boundary_ref, sems):
    leaf_count = out_ref.shape[0]
    copies = []
    for step in range(leaf_count // group):
        leaves = pl.ds(step * group, group)
        parts = (
            (inverse_hbm.at[leaves], inverse_ref.at[leaves]),
            (boundary_hbm.at[leaves], boundary_ref.at[leaves]),
        )
        copies.append(
            [pltpu.make_async_copy(a, b, sems.at[step, i]) for i, (a, b) in enumerate(parts)]
        )
        for copy in copies[-1]:
            copy.start()
    for step in range(leaf_count // group):
        for copy in copies[step]:
            copy.wait()
        for j in range(step * group, (step + 1) * group):
            out_ref[j] = rows_dot(boundary_ref[j], inverse_ref[j]).astype(BF16)


def near_kernel(state_ref, pick_ref, out_ref):
    out_ref[...] = jnp.dot(
        state_ref[...], pick_ref[: state_ref.shape[1], :], preferred_element_type=F32
    ).astype(BF16)


def leaf_kernel(
    group,
    beside_ref,
    picked_ref,
    pick_ref,
    matrix_ref,
    interior_ref,
    top_ref,
    out_hbm,
    top_hbm,
    out_ref,
    top_sem,
    sems,
):
    leaf_count, edge, leaf_size = matrix_ref.shape
    rows = beside_ref.shape[1]
    beside = beside_ref[...]
    copies = [pltpu.make_async_copy(top_ref, top_hbm, top_sem)]
    copies[0].start()
    for step in range(leaf_count // group):
        first = step * group
        span = slice(first * edge, (first + group) * edge)
        picked = jnp.dot(beside, pick_ref[2 * rows :, span], preferred_element_type=F32)
        picked = (picked + picked_ref[:, span].astype(F32)).astype(BF16)
        for g in range(group):
            lanes = slice((first + g) * leaf_size, (first + g + 1) * leaf_size)
            lifted = jnp.dot(
                picked[:, g * edge : (g + 1) * edge],
                matrix_ref[first + g],
                preferred_element_type=F32,
            )
            out_ref[:, lanes] = (interior_ref[:, lanes].astype(F32) - lifted).astype(BF16)
        lanes = pl.ds(first * leaf_size, group * leaf_size)
        copies.append(
            pltpu.make_async_copy(out_ref.at[:, lanes], out_hbm.at[:, lanes], sems.at[step])
        )
        copies[-1].start()
    for copy in copies:
        copy.wait()


def half_copies(which, inverse_hbm, to_ref, sems):
    pairs, pieces = sems.shape
    span = to_ref.shape[1] // pairs
    tall = to_ref.shape[0] // pieces
    copies = []
    for q in range(pairs):
        start = pl.multiple_of((pairs * which + q) * span, span)
        copies.append([])
        for r in range(pieces):
            here = pl.ds(r * tall, tall)
            copies[-1].append(
                pltpu.make_async_copy(
                    inverse_hbm.at[here, pl.ds(start, span)],
                    to_ref.at[here, pl.ds(q * span, span)],
                    sems.at[q, r],
                )
            )
            copies[-1][-1].start()
    return copies


def turn_kernel(inverse_hbm, taken_hbm, out_ref, kept_ref, taken_ref, kept_sems, taken_sems):
    core = own_place()[1]
    rows = taken_ref.shape[0]
    span = kept_ref.shape[1] // kept_sems.shape[0]
    taken_copies = []
    for q in range(taken_sems.shape[0]):
        lanes = pl.ds(q * span, span)
        taken_copies.append(
            pltpu.make_async_copy(taken_hbm.at[:, lanes], taken_ref.at[:, lanes], taken_sems.at[q])
        )
        taken_copies[-1].start()
    kept_copies = half_copies(own_half(), inverse_hbm, kept_ref, kept_sems)
    piece = min(span, 256)
    for q in range(len(kept_copies)):
        taken_copies[q].wait()
        for copy in kept_copies[q]:
            copy.wait()
        for k in range(q * span, (q + 1) * span, piece):
            kept = jnp.transpose(kept_ref[:, k : k + piece])
            taken = jnp.transpose(taken_ref[:, k : k + piece])

            @pl.when(core == 0)
            def _():
                out_ref[k : k + piece, :rows] = kept
                out_ref[k : k + piece, rows:] = taken

            @pl.when(core != 0)
            def _():
                out_ref[k : k + piece, :rows] = taken
                out_ref[k : k + piece, rows:] = kept


def fold_kernel(blocks, more, skipped, inverse_ref, *refs):
    refs = refs[skipped:]
    out_ref = refs[-1]
    wave_rows, rows = out_ref.shape
    chip = own_place()[0]
    half = inverse_ref.shape[0] // rows
    total = refs[-2][...] if more else jnp.zeros((wave_rows, rows), F32)
    for n, i in enumerate(blocks):
        place = pl.ds(pl.multiple_of(((chip % half) ^ i) * rows, rows), rows)
        total += jnp.dot(refs[n][...], inverse_ref[place, :], preferred_element_type=F32)
    out_ref[...] = total.astype(out_ref.dtype)


def join_kernel(
    turn, mine_ref, other_ref, state_ref, scale_ref, later_ref, next_ref, out_ref
):
    wave_rows = mine_ref.shape[0]
    last = lax.axis_index("panel") == lax.axis_size("panel") - 1
    forward, backward, wave = own_turn(turn)
    here = pl.ds(pl.multiple_of(wave * wave_rows, wave_rows), wave_rows)
    solved = (mine_ref[...].astype(F32) + other_ref[...].astype(F32)).astype(BF16).astype(F32)
    older = state_ref[here, :].astype(F32)
    field = (solved + jnp.where(backward, older, 0.0)).astype(BF16)
    scale = jnp.where(backward, scale_ref[1:2, :], scale_ref[0:1, :])
    ahead = jnp.where(forward & ~last, later_ref[here, :].astype(F32), 0.0)
    out_ref[...] = (scale * field.astype(F32) + ahead).astype(BF16)
    if turn == 0:

        @pl.when(last)
        def _():
            out_ref[...] = later_ref[wave_rows : 2 * wave_rows, :]

    @pl.when(forward | backward)
    def _():
        next_ref[here, :] = field


def turn_routes(turn, panels, waves):
    if turn == 0:
        return [(p, (p + 1) % panels) for p in range(panels)]
    at = [s if s < panels else 2 * (panels - 1) - s for s in range(2 * panels - 1)]
    pairs = []
    for wave in range(waves):
        step = turn - wave
        if 0 <= step < 2 * (panels - 1):
            pairs.append((at[step], at[step + 1]))
    sources = [a for a, _ in pairs]
    targets = [b for _, b in pairs]
    for panel in range(panels):
        if panel not in sources and panel not in targets:
            pairs.append((panel, panel))
    spare = [p for p in targets if p not in sources]
    unfed = [p for p in sources if p not in targets]
    return pairs + list(zip(spare, unfed))


def spread(values, panel_pairs, chips):
    half = chips // 2
    received = []
    for i in reversed(range(half)):
        route = []
        for start, end in panel_pairs:
            for chip in range(chips):
                for core in range(2):
                    there = chip ^ (half * core + i)
                    route.append(
                        (2 * (start * chips + chip) + core, 2 * (end * chips + there) + core)
                    )
        received.append(lax.ppermute(values, ("panel", "front"), route))
    return received[::-1]


def body(top_source, leaf_source, top_inverse, leaf_inverse, boundary, touch_rows, coupling):
    sources = top_source.shape[1]
    rows = top_source.shape[2]
    width = top_inverse.shape[2]
    leaf_count, leaf_size = leaf_inverse.shape[1:3]
    edge = boundary.shape[2]
    panels = lax.axis_size("panel")
    front = lax.axis_size("front")
    chips, half = front // 2, front // 4
    chip_rows = 2 * rows
    panel = lax.axis_index("panel")
    core = lax.axis_index("front") % 2
    wave_rows = sources // WAVES
    group = group_of(leaf_count, 6)
    steps = leaf_count // group
    all_lanes = leaf_count * leaf_size

    swap_core = [(i, i ^ 1) for i in range(front)]
    swap_chip = [(i, i + 1) for i in range(1, front - 1, 2)]
    swap_chip = swap_chip + [(j, i) for i, j in swap_chip]

    tile = group_of(leaf_count, 8 if leaf_count % 8 == 0 else 4)
    touch_rows = touch_rows.reshape(leaf_count // tile, tile, edge)
    pieces = group_of(rows // 16, 8)
    outward, partial, interior, given = pl.pallas_call(
        functools.partial(push_kernel, group),
        out_shape=(
            pltpu.VMEM((sources, rows), BF16),
            pltpu.VMEM((sources, chip_rows), F32),
            pltpu.VMEM((sources, all_lanes), BF16),
            pltpu.VMEM((rows, width // 2), BF16),
        ),
        in_specs=[VMEM] * 2 + [ANY] * 4,
        out_specs=(VMEM, VMEM, VMEM, VMEM),
        scratch_shapes=[
            pltpu.VMEM((sources, all_lanes), BF16),
            pltpu.VMEM((leaf_count, leaf_size, leaf_size), BF16),
            pltpu.VMEM((leaf_count, edge, leaf_size), BF16),
            pltpu.VMEM((2, group * edge, 3 * rows), BF16),
            pltpu.VMEM((sources, 3 * rows), F32),
            pltpu.SemaphoreType.DMA((half, pieces)),
            pltpu.SemaphoreType.DMA((steps, 3)),
        ],
        compiler_params=params(24),
    )(
        touch_rows,
        top_source,
        in_hbm(leaf_source[0]),
        in_hbm(leaf_inverse[0]),
        in_hbm(boundary[0]),
        in_hbm(top_inverse[0]),
    )
    coupling, given, outward = lax.optimization_barrier((coupling, given, outward))
    taken = lax.ppermute(given, "front", swap_core)
    inward = lax.ppermute(outward, "front", swap_chip)
    ring = [((p + 1) % panels, p) for p in range(panels)]
    later = lax.ppermute(coupling, "panel", ring)
    inward, later = lax.optimization_barrier((inward, later))
    forward_scale = jnp.where(panel == panels - 1, coupling, later)
    scales = jnp.concatenate([forward_scale, coupling], axis=0)
    blank = jnp.zeros_like(partial[:, :rows])
    whole_inward = jnp.where(
        core == 0,
        jnp.concatenate([inward.astype(F32), blank], axis=1),
        jnp.concatenate([blank, inward.astype(F32)], axis=1),
    )
    partial = (partial - whole_inward).astype(BF16)
    partner = lax.ppermute(partial, "front", swap_core)
    partner_scales = lax.ppermute(scales, "front", swap_core)
    known = (partial.astype(F32) + partner.astype(F32)).astype(BF16)
    scales = jnp.where(
        core == 0,
        jnp.concatenate([scales, partner_scales], axis=1),
        jnp.concatenate([partner_scales, scales], axis=1),
    )
    scales = in_vmem(scales)
    arrived = [in_vmem(a) for a in spread(known[:wave_rows], [(0, 0)], chips)]
    later_known = in_vmem(lax.ppermute(known, "panel", ring))

    inverse = pl.pallas_call(
        turn_kernel,
        out_shape=pltpu.VMEM((width // 2, chip_rows), BF16),
        in_specs=[ANY, ANY],
        out_specs=VMEM,
        scratch_shapes=[
            pltpu.VMEM((rows, width // 2), BF16),
            pltpu.VMEM((rows, width // 2), BF16),
            pltpu.SemaphoreType.DMA((half, pieces)),
            pltpu.SemaphoreType.DMA((half,)),
        ],
        compiler_params=params(8),
        cost_estimate=pl.CostEstimate(
            flops=2 * sources * width * rows, bytes_accessed=4 * width * rows, transcendentals=0
        ),
    )(in_hbm(top_inverse[0]), taken)
    inverse = in_vmem(inverse)

    state = jnp.zeros((sources, chip_rows), BF16)
    turns = 2 * (panels - 1) + WAVES
    extra = []
    for turn in range(turns):
        share = ()
        halves = (range(half // 2, half), range(half // 2)) if turn else (range(half),)
        for blocks in halves:
            last = blocks is halves[-1]
            behind = extra if last else []
            operands = [arrived[i] for i in blocks] + [in_vmem(v) for v in share]
            share = (
                pl.pallas_call(
                    functools.partial(fold_kernel, blocks, bool(share), len(behind)),
                    out_shape=pltpu.VMEM((wave_rows, chip_rows), BF16 if last else F32),
                    in_specs=[VMEM] + [ANY] * len(behind) + [VMEM] * len(operands),
                    out_specs=VMEM,
                    compiler_params=params(4),
                )(inverse, *behind, *operands),
            )
        share, extra = share[0], []
        other = lax.ppermute(share, "front", swap_core)
        state, outgoing = pl.pallas_call(
            functools.partial(join_kernel, turn),
            out_shape=(
                pltpu.VMEM((sources, chip_rows), BF16),
                pltpu.VMEM((wave_rows, chip_rows), BF16),
            ),
            in_specs=[VMEM] * 5,
            out_specs=(VMEM, VMEM),
            input_output_aliases={2: 0},
            compiler_params=params(4),
        )(in_vmem(share), in_vmem(other), in_vmem(state), scales, later_known)
        if turn < turns - 1:
            routes = turn_routes(turn, panels, WAVES)
            arrived = [in_vmem(a) for a in spread(outgoing, routes, chips)]
        if turn == 1:
            picks = pl.pallas_call(
                pick_kernel,
                out_shape=pltpu.VMEM((3 * rows, leaf_count * edge), BF16),
                in_specs=[VMEM, ANY],
                out_specs=VMEM,
                compiler_params=params(4),
                cost_estimate=pl.CostEstimate(
                    flops=4 * sources * rows * leaf_count * edge,
                    bytes_accessed=6 * rows * leaf_count * edge,
                    transcendentals=0,
                ),
            )(touch_rows, outgoing)
            extra = [in_vmem(picks)]
        if turn == 2:
            matrices = pl.pallas_call(
                functools.partial(lift_matrix_kernel, group),
                out_shape=pltpu.VMEM((leaf_count, edge, leaf_size), BF16),
                in_specs=[ANY, ANY, ANY],
                out_specs=VMEM,
                scratch_shapes=[
                    pltpu.VMEM((leaf_count, leaf_size, leaf_size), BF16),
                    pltpu.VMEM((leaf_count, edge, leaf_size), BF16),
                    pltpu.SemaphoreType.DMA((steps, 2)),
                ],
                compiler_params=params(12),
                cost_estimate=pl.CostEstimate(
                    flops=2 * leaf_count * edge * leaf_size * leaf_size,
                    bytes_accessed=4 * leaf_count * leaf_size * leaf_size,
                    transcendentals=0,
                ),
            )(in_hbm(leaf_inverse[0]), in_hbm(boundary[0]), outgoing)
            extra = [in_vmem(matrices)]

    top_field = jnp.where(core == 0, state[:, :rows], state[:, rows:])
    beside = lax.ppermute(top_field, "front", swap_chip)
    picked = pl.pallas_call(
        near_kernel,
        out_shape=pltpu.VMEM((sources, leaf_count * edge), BF16),
        in_specs=[VMEM] * 2,
        out_specs=VMEM,
        compiler_params=params(8),
        cost_estimate=pl.CostEstimate(
            flops=4 * sources * rows * leaf_count * edge,
            bytes_accessed=4 * rows * leaf_count * edge,
            transcendentals=0,
        ),
    )(in_vmem(state), in_vmem(picks))
    leaf_field, top_field = pl.pallas_call(
        functools.partial(leaf_kernel, group),
        out_shape=(
            jax.ShapeDtypeStruct((sources, all_lanes), BF16),
            jax.ShapeDtypeStruct((sources, rows), BF16),
        ),
        in_specs=[VMEM] * 6,
        out_specs=(ANY, ANY),
        scratch_shapes=[
            pltpu.VMEM((sources, all_lanes), BF16),
            pltpu.SemaphoreType.DMA,
            pltpu.SemaphoreType.DMA((steps,)),
        ],
        compiler_params=params(8),
    )(in_vmem(beside), in_vmem(picked), in_vmem(picks), in_vmem(matrices), in_vmem(interior), in_vmem(top_field))
    return (top_field[None], leaf_field[None])


def solution(mesh):
    placed = (
        P("panel", None, "front"),
        P("panel", None, "front"),
        P("panel", "front", None),
        P("panel", "front", None, None),
        P("panel", "front", None, None),
        P("panel", "front", None),
        P("panel", "front"),
    )
    return jax.shard_map(
        body,
        mesh=mesh,
        in_specs=placed,
        out_specs=(P("panel", None, "front"), P("panel", None, "front")),
        check_vma=False,
    )
```

```python
import functools

import jax
import jax.numpy as jnp
from jax import lax
from jax.experimental import pallas as pl
from jax.experimental.pallas import tpu as pltpu
from jax.sharding import PartitionSpec as P

WAVES = 2
F32 = jnp.float32
BF16 = jnp.bfloat16
VMEM = pl.BlockSpec(memory_space=pltpu.VMEM)
ANY = pl.BlockSpec(memory_space=pl.ANY)


def params(mib):
    return pltpu.CompilerParams(vmem_limit_bytes=mib * 1024 * 1024)


def in_vmem(value):
    return pltpu.with_memory_space_constraint(value, pltpu.VMEM)


def in_hbm(value):
    return pltpu.with_memory_space_constraint(value, pltpu.HBM)


def rows_dot(left, right):
    return lax.dot_general(left, right, (((1,), (1,)), ((), ())), preferred_element_type=F32)


def group_of(leaf_count, most):
    return max(g for g in range(1, most + 1) if leaf_count % g == 0)


def own_place():
    place = lax.axis_index("front")
    return place // 2, place % 2


def own_half():
    chip, core = own_place()
    return (chip // (lax.axis_size("front") // 4)) ^ core


def own_turn(turn):
    panel = lax.axis_index("panel")
    panels = lax.axis_size("panel")
    up_wave = turn - panel
    down_wave = turn - (2 * (panels - 1) - panel)
    up = (up_wave >= 0) & (up_wave < WAVES)
    down = (down_wave >= 0) & (down_wave < WAVES) & (panel < panels - 1)
    wave = jnp.where(up, up_wave, jnp.where(down, down_wave, 0))
    return up, down, wave


def push_kernel(
    group,
    rows_ref,
    source_hbm,
    inverse_hbm,
    boundary_hbm,
    solver_hbm,
    outward_ref,
    partial_ref,
    interior_ref,
    given_ref,
    source_ref,
    inverse_ref,
    boundary_ref,
    pick_ref,
    total_ref,
    half_sems,
    sems,
):
    leaf_count, leaf_size = inverse_ref.shape[:2]
    edge = boundary_ref.shape[1]
    rows = outward_ref.shape[1]
    window = 3 * rows
    core = own_place()[1]
    copies = []
    for step in range(leaf_count // group):
        leaves = pl.ds(step * group, group)
        lanes = pl.ds(step * group * leaf_size, group * leaf_size)
        parts = (
            (source_hbm.at[:, lanes], source_ref.at[:, lanes]),
            (inverse_hbm.at[leaves], inverse_ref.at[leaves]),
            (boundary_hbm.at[leaves], boundary_ref.at[leaves]),
        )
        copies.append(
            [pltpu.make_async_copy(a, b, sems.at[step, i]) for i, (a, b) in enumerate(parts)]
        )
        for copy in copies[-1]:
            copy.start()
    staged = sum(half_copies(1 - own_half(), solver_hbm, given_ref, half_sems), [])
    places = lax.broadcasted_iota(jnp.int16, (edge, window), 1)
    for step in range(leaf_count // group):
        for copy in copies[step]:
            copy.wait()
        first = step * group
        interior = []
        for j in range(first, first + group):
            lanes = slice(j * leaf_size, (j + 1) * leaf_size)
            interior.append(rows_dot(source_ref[:, lanes], inverse_ref[j]).astype(BF16))
            interior_ref[:, lanes] = interior[-1]
        pushed = [
            rows_dot(interior[g], boundary_ref[first + g]).astype(BF16) for g in range(group)
        ]
        if step == 0:
            lines = [rows_ref[i] for i in range(rows_ref.shape[0])]
            if leaf_count % 8:
                lines.append(jnp.zeros((-leaf_count % 8, edge), jnp.int32))
            local = jnp.concatenate(lines, axis=0) - (lax.axis_index("front") - 1) * rows
            columns = jnp.transpose(local).astype(jnp.int16)
        for g in range(group):
            pick_ref[step % 2, g * edge : (g + 1) * edge, :] = jnp.where(
                columns[:, first + g : first + g + 1] == places, jnp.bfloat16(1), jnp.bfloat16(0)
            )
        total = jnp.dot(
            jnp.concatenate(pushed, axis=1), pick_ref[step % 2], preferred_element_type=F32
        )
        if step == 0:
            total_ref[...] = total
        else:
            total_ref[...] += total
    for copy in staged:
        copy.wait()
    @pl.when(core == 0)
    def _():
        outward_ref[...] = total_ref[:, :rows].astype(BF16)
        partial_ref[...] = total_ref[:, rows:]

    @pl.when(core != 0)
    def _():
        outward_ref[...] = total_ref[:, 2 * rows :].astype(BF16)
        partial_ref[...] = total_ref[:, : 2 * rows]


def prepare_kernel(
    group, panels, given, rows_ref, inverse_hbm, boundary_hbm, after_ref, *refs
):
    picks_ref, matrix_ref, inverse_ref, boundary_ref, sems = refs[given:]
    tile, edge = rows_ref.shape[1:]
    leaf_count = rows_ref.shape[0] * tile
    window = picks_ref.shape[0]
    rows = window // 3
    panel = lax.axis_index("panel")
    place = lax.axis_index("front")
    chosen = panel == panels[0]
    for other in panels[1:]:
        chosen = chosen | (panel == other)

    @pl.when(chosen)
    def _():
        copies = []
        for step in range(leaf_count // group):
            leaves = pl.ds(step * group, group)
            parts = (
                (inverse_hbm.at[leaves], inverse_ref.at[leaves]),
                (boundary_hbm.at[leaves], boundary_ref.at[leaves]),
            )
            copies.append(
                [pltpu.make_async_copy(a, b, sems.at[step, i]) for i, (a, b) in enumerate(parts)]
            )
            for copy in copies[-1]:
                copy.start()
        local = rows_ref[...] - (place - 1) * rows
        shifted = jnp.where(local < rows, local + 2 * rows, local - rows)
        local = jnp.where(place % 2 == 0, shifted, local)
        places = lax.broadcasted_iota(jnp.int16, (window, edge), 0)
        for j in range(leaf_count):
            picks_ref[:, j * edge : (j + 1) * edge] = jnp.where(
                local[j // tile, j % tile : j % tile + 1, :].astype(jnp.int16) == places,
                jnp.bfloat16(1),
                jnp.bfloat16(0),
            )
        for step in range(leaf_count // group):
            for copy in copies[step]:
                copy.wait()
            for j in range(step * group, (step + 1) * group):
                matrix_ref[j] = rows_dot(boundary_ref[j], inverse_ref[j]).astype(BF16)


def near_kernel(state_ref, pick_ref, out_ref):
    out_ref[...] = jnp.dot(
        state_ref[...], pick_ref[: state_ref.shape[1], :], preferred_element_type=F32
    ).astype(BF16)


def leaf_kernel(
    group,
    beside_ref,
    picked_ref,
    pick_ref,
    matrix_ref,
    interior_ref,
    top_ref,
    out_hbm,
    top_hbm,
    out_ref,
    top_sem,
    sems,
):
    leaf_count, edge, leaf_size = matrix_ref.shape
    rows = beside_ref.shape[1]
    beside = beside_ref[...]
    copies = [pltpu.make_async_copy(top_ref, top_hbm, top_sem)]
    copies[0].start()
    for step in range(leaf_count // group):
        first = step * group
        span = slice(first * edge, (first + group) * edge)
        picked = jnp.dot(beside, pick_ref[2 * rows :, span], preferred_element_type=F32)
        picked = (picked + picked_ref[:, span].astype(F32)).astype(BF16)
        for g in range(group):
            lanes = slice((first + g) * leaf_size, (first + g + 1) * leaf_size)
            lifted = jnp.dot(
                picked[:, g * edge : (g + 1) * edge],
                matrix_ref[first + g],
                preferred_element_type=F32,
            )
            out_ref[:, lanes] = (interior_ref[:, lanes].astype(F32) - lifted).astype(BF16)
        lanes = pl.ds(first * leaf_size, group * leaf_size)
        copies.append(
            pltpu.make_async_copy(out_ref.at[:, lanes], out_hbm.at[:, lanes], sems.at[step])
        )
        copies[-1].start()
    for copy in copies:
        copy.wait()


def half_copies(which, inverse_hbm, to_ref, sems):
    pairs, pieces = sems.shape
    span = to_ref.shape[1] // pairs
    tall = to_ref.shape[0] // pieces
    copies = []
    for q in range(pairs):
        start = pl.multiple_of((pairs * which + q) * span, span)
        copies.append([])
        for r in range(pieces):
            here = pl.ds(r * tall, tall)
            copies[-1].append(
                pltpu.make_async_copy(
                    inverse_hbm.at[here, pl.ds(start, span)],
                    to_ref.at[here, pl.ds(q * span, span)],
                    sems.at[q, r],
                )
            )
            copies[-1][-1].start()
    return copies


def turn_kernel(inverse_hbm, taken_hbm, out_ref, kept_ref, taken_ref, kept_sems, taken_sems):
    core = own_place()[1]
    rows = taken_ref.shape[0]
    span = kept_ref.shape[1] // kept_sems.shape[0]
    taken_copies = []
    for q in range(taken_sems.shape[0]):
        lanes = pl.ds(q * span, span)
        taken_copies.append(
            pltpu.make_async_copy(taken_hbm.at[:, lanes], taken_ref.at[:, lanes], taken_sems.at[q])
        )
        taken_copies[-1].start()
    kept_copies = half_copies(own_half(), inverse_hbm, kept_ref, kept_sems)
    piece = min(span, 256)
    for q in range(len(kept_copies)):
        taken_copies[q].wait()
        for copy in kept_copies[q]:
            copy.wait()
        for k in range(q * span, (q + 1) * span, piece):
            kept = jnp.transpose(kept_ref[:, k : k + piece])
            taken = jnp.transpose(taken_ref[:, k : k + piece])

            @pl.when(core == 0)
            def _():
                out_ref[k : k + piece, :rows] = kept
                out_ref[k : k + piece, rows:] = taken

            @pl.when(core != 0)
            def _():
                out_ref[k : k + piece, :rows] = taken
                out_ref[k : k + piece, rows:] = kept


def fold_kernel(blocks, more, skipped, inverse_ref, *refs):
    refs = refs[skipped:]
    out_ref = refs[-1]
    wave_rows, rows = out_ref.shape
    chip = own_place()[0]
    half = inverse_ref.shape[0] // rows
    total = refs[-2][...] if more else jnp.zeros((wave_rows, rows), F32)
    for n, i in enumerate(blocks):
        place = pl.ds(pl.multiple_of(((chip % half) ^ i) * rows, rows), rows)
        total += jnp.dot(refs[n][...], inverse_ref[place, :], preferred_element_type=F32)
    out_ref[...] = total.astype(out_ref.dtype)


def join_kernel(
    turn, mine_ref, other_ref, state_ref, scale_ref, later_ref, next_ref, out_ref
):
    wave_rows = mine_ref.shape[0]
    last = lax.axis_index("panel") == lax.axis_size("panel") - 1
    forward, backward, wave = own_turn(turn)
    here = pl.ds(pl.multiple_of(wave * wave_rows, wave_rows), wave_rows)
    solved = (mine_ref[...].astype(F32) + other_ref[...].astype(F32)).astype(BF16).astype(F32)
    older = state_ref[here, :].astype(F32)
    field = (solved + jnp.where(backward, older, 0.0)).astype(BF16)
    scale = jnp.where(backward, scale_ref[1:2, :], scale_ref[0:1, :])
    ahead = jnp.where(forward & ~last, later_ref[here, :].astype(F32), 0.0)
    out_ref[...] = (scale * field.astype(F32) + ahead).astype(BF16)
    if turn == 0:

        @pl.when(last)
        def _():
            out_ref[...] = later_ref[wave_rows : 2 * wave_rows, :]

    @pl.when(forward | backward)
    def _():
        next_ref[here, :] = field


def last_join_kernel(turn, mine_ref, other_ref, state_ref, next_ref, top_ref):
    wave_rows = mine_ref.shape[0]
    rows = top_ref.shape[1]
    forward, backward, wave = own_turn(turn)
    here = pl.ds(pl.multiple_of(wave * wave_rows, wave_rows), wave_rows)
    solved = (mine_ref[...].astype(F32) + other_ref[...].astype(F32)).astype(BF16).astype(F32)
    older = state_ref[here, :].astype(F32)

    @pl.when(forward | backward)
    def _():
        next_ref[here, :] = (solved + jnp.where(backward, older, 0.0)).astype(BF16)

    @pl.when(own_place()[1] == 0)
    def _():
        top_ref[...] = next_ref[:, :rows]

    @pl.when(own_place()[1] != 0)
    def _():
        top_ref[...] = next_ref[:, rows:]


def turn_routes(turn, panels, waves):
    if turn == 0:
        return [(p, (p + 1) % panels) for p in range(panels)]
    at = [s if s < panels else 2 * (panels - 1) - s for s in range(2 * panels - 1)]
    pairs = []
    for wave in range(waves):
        step = turn - wave
        if 0 <= step < 2 * (panels - 1):
            pairs.append((at[step], at[step + 1]))
    sources = [a for a, _ in pairs]
    targets = [b for _, b in pairs]
    for panel in range(panels):
        if panel not in sources and panel not in targets:
            pairs.append((panel, panel))
    spare = [p for p in targets if p not in sources]
    unfed = [p for p in sources if p not in targets]
    return pairs + list(zip(spare, unfed))


def preparing_turns(panels):
    turns = range(1, 2 * (panels - 1) + WAVES - 1)
    alone = {t: [p for p, q in turn_routes(t, panels, WAVES) if p == q] for t in turns}
    chosen = {}
    left = list(range(panels))
    while left:
        turn = max(turns, key=lambda t: sum(p in left for p in alone[t]))
        found = [p for p in left if p in alone[turn]] or left
        chosen[turn] = chosen.get(turn, []) + found
        left = [p for p in left if p not in found]
    return chosen


def spread(values, panel_pairs, chips):
    half = chips // 2
    received = []
    for i in reversed(range(half)):
        route = []
        for start, end in panel_pairs:
            for chip in range(chips):
                for core in range(2):
                    there = chip ^ (half * core + i)
                    route.append(
                        (2 * (start * chips + chip) + core, 2 * (end * chips + there) + core)
                    )
        received.append(lax.ppermute(values, ("panel", "front"), route))
    return received[::-1]


def body(top_source, leaf_source, top_inverse, leaf_inverse, boundary, touch_rows, coupling):
    sources = top_source.shape[1]
    rows = top_source.shape[2]
    width = top_inverse.shape[2]
    leaf_count, leaf_size = leaf_inverse.shape[1:3]
    edge = boundary.shape[2]
    panels = lax.axis_size("panel")
    front = lax.axis_size("front")
    chips, half = front // 2, front // 4
    chip_rows = 2 * rows
    panel = lax.axis_index("panel")
    core = lax.axis_index("front") % 2
    wave_rows = sources // WAVES
    group = group_of(leaf_count, 6)
    steps = leaf_count // group
    all_lanes = leaf_count * leaf_size

    swap_core = [(i, i ^ 1) for i in range(front)]
    swap_chip = [(i, i + 1) for i in range(1, front - 1, 2)]
    swap_chip = swap_chip + [(j, i) for i, j in swap_chip]

    tile = group_of(leaf_count, 8 if leaf_count % 8 == 0 else 4)
    touch_rows = touch_rows.reshape(leaf_count // tile, tile, edge)
    pieces = group_of(rows // 16, 8)
    outward, partial, interior, given = pl.pallas_call(
        functools.partial(push_kernel, group),
        out_shape=(
            pltpu.VMEM((sources, rows), BF16),
            pltpu.VMEM((sources, chip_rows), F32),
            pltpu.VMEM((sources, all_lanes), BF16),
            pltpu.VMEM((rows, width // 2), BF16),
        ),
        in_specs=[VMEM] + [ANY] * 4,
        out_specs=(VMEM, VMEM, VMEM, VMEM),
        scratch_shapes=[
            pltpu.VMEM((sources, all_lanes), BF16),
            pltpu.VMEM((leaf_count, leaf_size, leaf_size), BF16),
            pltpu.VMEM((leaf_count, edge, leaf_size), BF16),
            pltpu.VMEM((2, group * edge, 3 * rows), BF16),
            pltpu.VMEM((sources, 3 * rows), F32),
            pltpu.SemaphoreType.DMA((half, pieces)),
            pltpu.SemaphoreType.DMA((steps, 3)),
        ],
        compiler_params=params(24),
    )(
        touch_rows,
        in_hbm(leaf_source[0]),
        in_hbm(leaf_inverse[0]),
        in_hbm(boundary[0]),
        in_hbm(top_inverse[0]),
    )
    coupling, given, outward = lax.optimization_barrier((coupling, given, outward))
    taken = lax.ppermute(given, "front", swap_core)
    inward = lax.ppermute(outward, "front", swap_chip)
    ring = [((p + 1) % panels, p) for p in range(panels)]
    later = lax.ppermute(coupling, "panel", ring)
    inward, later = lax.optimization_barrier((inward, later))
    forward_scale = jnp.where(panel == panels - 1, coupling, later)
    scales = jnp.concatenate([forward_scale, coupling], axis=0)
    own_part = top_source[0].astype(F32) - inward.astype(F32)
    blank = jnp.zeros_like(own_part)
    own_part = jnp.where(
        core == 0,
        jnp.concatenate([own_part, blank], axis=1),
        jnp.concatenate([blank, own_part], axis=1),
    )
    partial = (own_part - partial).astype(BF16)
    partner = lax.ppermute(partial, "front", swap_core)
    partner_scales = lax.ppermute(scales, "front", swap_core)
    known = (partial.astype(F32) + partner.astype(F32)).astype(BF16)
    scales = jnp.where(
        core == 0,
        jnp.concatenate([scales, partner_scales], axis=1),
        jnp.concatenate([partner_scales, scales], axis=1),
    )
    scales = in_vmem(scales)
    arrived = [in_vmem(a) for a in spread(known[:wave_rows], [(0, 0)], chips)]
    later_known = in_vmem(lax.ppermute(known, "panel", ring))

    inverse = pl.pallas_call(
        turn_kernel,
        out_shape=pltpu.VMEM((width // 2, chip_rows), BF16),
        in_specs=[ANY, ANY],
        out_specs=VMEM,
        scratch_shapes=[
            pltpu.VMEM((rows, width // 2), BF16),
            pltpu.VMEM((rows, width // 2), BF16),
            pltpu.SemaphoreType.DMA((half, pieces)),
            pltpu.SemaphoreType.DMA((half,)),
        ],
        compiler_params=params(8),
        cost_estimate=pl.CostEstimate(
            flops=2 * sources * width * rows, bytes_accessed=4 * width * rows, transcendentals=0
        ),
    )(in_hbm(top_inverse[0]), taken)
    inverse = in_vmem(inverse)

    state = jnp.zeros((sources, chip_rows), BF16)
    turns = 2 * (panels - 1) + WAVES
    extra, made = [], []
    preparing = preparing_turns(panels)
    for turn in range(turns):
        share = ()
        halves = (range(half // 2, half), range(half // 2)) if turn else (range(half),)
        for blocks in halves:
            last = blocks is halves[-1]
            behind = extra if last else []
            operands = [arrived[i] for i in blocks] + [in_vmem(v) for v in share]
            share = (
                pl.pallas_call(
                    functools.partial(fold_kernel, blocks, bool(share), len(behind)),
                    out_shape=pltpu.VMEM((wave_rows, chip_rows), BF16 if last else F32),
                    in_specs=[VMEM] + [ANY] * len(behind) + [VMEM] * len(operands),
                    out_specs=VMEM,
                    compiler_params=params(4),
                )(inverse, *behind, *operands),
            )
        share, extra = share[0], []
        other = lax.ppermute(share, "front", swap_core)
        if turn == turns - 1:
            state, top_field = pl.pallas_call(
                functools.partial(last_join_kernel, turn),
                out_shape=(
                    pltpu.VMEM((sources, chip_rows), BF16),
                    pltpu.VMEM((sources, rows), BF16),
                ),
                in_specs=[VMEM] * 3,
                out_specs=(VMEM, VMEM),
                input_output_aliases={2: 0},
                compiler_params=params(4),
            )(in_vmem(share), in_vmem(other), in_vmem(state))
            break
        state, outgoing = pl.pallas_call(
            functools.partial(join_kernel, turn),
            out_shape=(
                pltpu.VMEM((sources, chip_rows), BF16),
                pltpu.VMEM((wave_rows, chip_rows), BF16),
            ),
            in_specs=[VMEM] * 5,
            out_specs=(VMEM, VMEM),
            input_output_aliases={2: 0},
            compiler_params=params(4),
        )(in_vmem(share), in_vmem(other), in_vmem(state), scales, later_known)
        routes = turn_routes(turn, panels, WAVES)
        arrived = [in_vmem(a) for a in spread(outgoing, routes, chips)]
        if turn in preparing:
            made = pl.pallas_call(
                functools.partial(prepare_kernel, group, preparing[turn], len(made)),
                out_shape=(
                    pltpu.VMEM((3 * rows, leaf_count * edge), BF16),
                    pltpu.VMEM((leaf_count, edge, leaf_size), BF16),
                ),
                in_specs=[VMEM] + [ANY] * (3 + len(made)),
                out_specs=(VMEM, VMEM),
                input_output_aliases={4 + i: i for i in range(len(made))},
                scratch_shapes=[
                    pltpu.VMEM((leaf_count, leaf_size, leaf_size), BF16),
                    pltpu.VMEM((leaf_count, edge, leaf_size), BF16),
                    pltpu.SemaphoreType.DMA((steps, 2)),
                ],
                compiler_params=params(12),
                cost_estimate=pl.CostEstimate(
                    flops=8 * sources * rows * leaf_count * edge,
                    bytes_accessed=6 * rows * leaf_count * edge,
                    transcendentals=0,
                ),
            )(touch_rows, in_hbm(leaf_inverse[0]), in_hbm(boundary[0]), outgoing, *made)
            made = [in_vmem(m) for m in made]
            extra = made
    picks, matrices = made

    beside = lax.ppermute(top_field, "front", swap_chip)
    picked = pl.pallas_call(
        near_kernel,
        out_shape=pltpu.VMEM((sources, leaf_count * edge), BF16),
        in_specs=[VMEM] * 2,
        out_specs=VMEM,
        compiler_params=params(8),
        cost_estimate=pl.CostEstimate(
            flops=4 * sources * rows * leaf_count * edge,
            bytes_accessed=4 * rows * leaf_count * edge,
            transcendentals=0,
        ),
    )(in_vmem(state), in_vmem(picks))
    leaf_field, top_field = pl.pallas_call(
        functools.partial(leaf_kernel, group),
        out_shape=(
            jax.ShapeDtypeStruct((sources, all_lanes), BF16),
            jax.ShapeDtypeStruct((sources, rows), BF16),
        ),
        in_specs=[VMEM] * 6,
        out_specs=(ANY, ANY),
        scratch_shapes=[
            pltpu.VMEM((sources, all_lanes), BF16),
            pltpu.SemaphoreType.DMA,
            pltpu.SemaphoreType.DMA((steps,)),
        ],
        compiler_params=params(8),
    )(in_vmem(beside), in_vmem(picked), in_vmem(picks), in_vmem(matrices), in_vmem(interior), in_vmem(top_field))
    return (top_field[None], leaf_field[None])


def solution(mesh):
    placed = (
        P("panel", None, "front"),
        P("panel", None, "front"),
        P("panel", "front", None),
        P("panel", "front", None, None),
        P("panel", "front", None, None),
        P("panel", "front", None),
        P("panel", "front"),
    )
    return jax.shard_map(
        body,
        mesh=mesh,
        in_specs=placed,
        out_specs=(P("panel", None, "front"), P("panel", None, "front")),
        check_vma=False,
    )
```

```python
import functools

import jax
import jax.numpy as jnp
from jax import lax
from jax.experimental import pallas as pl
from jax.experimental.pallas import tpu as pltpu
from jax.sharding import PartitionSpec as P

WAVES = 2
F32 = jnp.float32
BF16 = jnp.bfloat16
VMEM = pl.BlockSpec(memory_space=pltpu.VMEM)
ANY = pl.BlockSpec(memory_space=pl.ANY)


def params(mib):
    return pltpu.CompilerParams(vmem_limit_bytes=mib * 1024 * 1024)


def in_vmem(value):
    return pltpu.with_memory_space_constraint(value, pltpu.VMEM)


def in_hbm(value):
    return pltpu.with_memory_space_constraint(value, pltpu.HBM)


def rows_dot(left, right):
    return lax.dot_general(left, right, (((1,), (1,)), ((), ())), preferred_element_type=F32)


def group_of(leaf_count, most):
    return max(g for g in range(1, most + 1) if leaf_count % g == 0)


def own_place():
    place = lax.axis_index("front")
    return place // 2, place % 2


def own_half():
    chip, core = own_place()
    return (chip // (lax.axis_size("front") // 4)) ^ core


def own_turn(turn):
    panel = lax.axis_index("panel")
    panels = lax.axis_size("panel")
    up_wave = turn - panel
    down_wave = turn - (2 * (panels - 1) - panel)
    up = (up_wave >= 0) & (up_wave < WAVES)
    down = (down_wave >= 0) & (down_wave < WAVES) & (panel < panels - 1)
    wave = jnp.where(up, up_wave, jnp.where(down, down_wave, 0))
    return up, down, wave


def push_kernel(
    group,
    rows_ref,
    source_hbm,
    inverse_hbm,
    boundary_hbm,
    solver_hbm,
    outward_ref,
    partial_ref,
    interior_ref,
    given_ref,
    source_ref,
    inverse_ref,
    boundary_ref,
    pick_ref,
    total_ref,
    half_sems,
    sems,
):
    leaf_count, leaf_size = inverse_ref.shape[:2]
    edge = boundary_ref.shape[1]
    rows = outward_ref.shape[1]
    window = 3 * rows
    core = own_place()[1]
    copies = []
    for step in range(leaf_count // group):
        leaves = pl.ds(step * group, group)
        lanes = pl.ds(step * group * leaf_size, group * leaf_size)
        parts = (
            (source_hbm.at[:, lanes], source_ref.at[:, lanes]),
            (inverse_hbm.at[leaves], inverse_ref.at[leaves]),
            (boundary_hbm.at[leaves], boundary_ref.at[leaves]),
        )
        copies.append(
            [pltpu.make_async_copy(a, b, sems.at[step, i]) for i, (a, b) in enumerate(parts)]
        )
        for copy in copies[-1]:
            copy.start()
    staged = sum(half_copies(1 - own_half(), solver_hbm, given_ref, half_sems), [])
    places = lax.broadcasted_iota(jnp.int16, (edge, window), 1)
    for step in range(leaf_count // group):
        for copy in copies[step]:
            copy.wait()
        first = step * group
        interior = []
        for j in range(first, first + group):
            lanes = slice(j * leaf_size, (j + 1) * leaf_size)
            interior.append(rows_dot(source_ref[:, lanes], inverse_ref[j]).astype(BF16))
            interior_ref[:, lanes] = interior[-1]
        pushed = [
            rows_dot(interior[g], boundary_ref[first + g]).astype(BF16) for g in range(group)
        ]
        if step == 0:
            lines = [rows_ref[i] for i in range(rows_ref.shape[0])]
            if leaf_count % 8:
                lines.append(jnp.zeros((-leaf_count % 8, edge), jnp.int32))
            local = jnp.concatenate(lines, axis=0) - (lax.axis_index("front") - 1) * rows
            columns = jnp.transpose(local).astype(jnp.int16)
        for g in range(group):
            pick_ref[step % 2, g * edge : (g + 1) * edge, :] = jnp.where(
                columns[:, first + g : first + g + 1] == places, jnp.bfloat16(1), jnp.bfloat16(0)
            )
        total = jnp.dot(
            jnp.concatenate(pushed, axis=1), pick_ref[step % 2], preferred_element_type=F32
        )
        if step == 0:
            total_ref[...] = total
        else:
            total_ref[...] += total
    for copy in staged:
        copy.wait()
    @pl.when(core == 0)
    def _():
        outward_ref[...] = total_ref[:, :rows].astype(BF16)
        partial_ref[...] = total_ref[:, rows:]

    @pl.when(core != 0)
    def _():
        outward_ref[...] = total_ref[:, 2 * rows :].astype(BF16)
        partial_ref[...] = total_ref[:, : 2 * rows]


def prepare_kernel(
    group, panels, given, rows_ref, inverse_hbm, boundary_hbm, after_ref, *refs
):
    picks_ref, matrix_ref, inverse_ref, boundary_ref, sems = refs[given:]
    tile, edge = rows_ref.shape[1:]
    leaf_count = rows_ref.shape[0] * tile
    window = picks_ref.shape[0]
    rows = window // 3
    panel = lax.axis_index("panel")
    place = lax.axis_index("front")
    chosen = panel == panels[0]
    for other in panels[1:]:
        chosen = chosen | (panel == other)

    @pl.when(chosen)
    def _():
        copies = []
        for step in range(leaf_count // group):
            leaves = pl.ds(step * group, group)
            parts = (
                (inverse_hbm.at[leaves], inverse_ref.at[leaves]),
                (boundary_hbm.at[leaves], boundary_ref.at[leaves]),
            )
            copies.append(
                [pltpu.make_async_copy(a, b, sems.at[step, i]) for i, (a, b) in enumerate(parts)]
            )
            for copy in copies[-1]:
                copy.start()
        local = rows_ref[...] - (place - 1) * rows
        shifted = jnp.where(local < rows, local + 2 * rows, local - rows)
        local = jnp.where(place % 2 == 0, shifted, local)
        places = lax.broadcasted_iota(jnp.int16, (window, edge), 0)
        for j in range(leaf_count):
            picks_ref[:, j * edge : (j + 1) * edge] = jnp.where(
                local[j // tile, j % tile : j % tile + 1, :].astype(jnp.int16) == places,
                jnp.bfloat16(1),
                jnp.bfloat16(0),
            )
        for step in range(leaf_count // group):
            for copy in copies[step]:
                copy.wait()
            for j in range(step * group, (step + 1) * group):
                matrix_ref[j] = rows_dot(boundary_ref[j], inverse_ref[j]).astype(BF16)


def near_kernel(state_ref, pick_ref, out_ref):
    out_ref[...] = jnp.dot(
        state_ref[...], pick_ref[: state_ref.shape[1], :], preferred_element_type=F32
    ).astype(BF16)


def leaf_kernel(
    group,
    beside_ref,
    picked_ref,
    pick_ref,
    matrix_ref,
    interior_ref,
    top_ref,
    out_hbm,
    top_hbm,
    all_ref,
    out_ref,
    top_sem,
    sems,
):
    leaf_count, edge, leaf_size = matrix_ref.shape
    rows = beside_ref.shape[1]
    copies = [pltpu.make_async_copy(top_ref, top_hbm, top_sem)]
    copies[0].start()
    picked = jnp.dot(beside_ref[...], pick_ref[2 * rows :, :], preferred_element_type=F32)
    all_ref[...] = (picked + picked_ref[...].astype(F32)).astype(BF16)
    for step in range(leaf_count // group):
        first = step * group
        for j in range(first, first + group):
            lanes = slice(j * leaf_size, (j + 1) * leaf_size)
            lifted = jnp.dot(
                all_ref[:, j * edge : (j + 1) * edge],
                matrix_ref[j],
                preferred_element_type=F32,
            )
            out_ref[:, lanes] = (interior_ref[:, lanes].astype(F32) - lifted).astype(BF16)
        lanes = pl.ds(first * leaf_size, group * leaf_size)
        copies.append(
            pltpu.make_async_copy(out_ref.at[:, lanes], out_hbm.at[:, lanes], sems.at[step])
        )
        copies[-1].start()
    for copy in copies:
        copy.wait()


def half_copies(which, inverse_hbm, to_ref, sems):
    pairs, pieces = sems.shape
    span = to_ref.shape[1] // pairs
    tall = to_ref.shape[0] // pieces
    copies = []
    for q in range(pairs):
        start = pl.multiple_of((pairs * which + q) * span, span)
        copies.append([])
        for r in range(pieces):
            here = pl.ds(r * tall, tall)
            copies[-1].append(
                pltpu.make_async_copy(
                    inverse_hbm.at[here, pl.ds(start, span)],
                    to_ref.at[here, pl.ds(q * span, span)],
                    sems.at[q, r],
                )
            )
            copies[-1][-1].start()
    return copies


def turn_kernel(inverse_hbm, taken_hbm, out_ref, kept_ref, taken_ref, kept_sems, taken_sems):
    core = own_place()[1]
    rows = taken_ref.shape[0]
    span = kept_ref.shape[1] // kept_sems.shape[0]
    taken_copies = []
    for q in range(taken_sems.shape[0]):
        lanes = pl.ds(q * span, span)
        taken_copies.append(
            pltpu.make_async_copy(taken_hbm.at[:, lanes], taken_ref.at[:, lanes], taken_sems.at[q])
        )
        taken_copies[-1].start()
    kept_copies = half_copies(own_half(), inverse_hbm, kept_ref, kept_sems)
    piece = min(span, 256)
    for q in range(len(kept_copies)):
        taken_copies[q].wait()
        for copy in kept_copies[q]:
            copy.wait()
        for k in range(q * span, (q + 1) * span, piece):
            kept = jnp.transpose(kept_ref[:, k : k + piece])
            taken = jnp.transpose(taken_ref[:, k : k + piece])

            @pl.when(core == 0)
            def _():
                out_ref[k : k + piece, :rows] = kept
                out_ref[k : k + piece, rows:] = taken

            @pl.when(core != 0)
            def _():
                out_ref[k : k + piece, :rows] = taken
                out_ref[k : k + piece, rows:] = kept


def fold_kernel(blocks, more, skipped, inverse_ref, *refs):
    refs = refs[skipped:]
    out_ref = refs[-1]
    wave_rows, rows = out_ref.shape
    chip = own_place()[0]
    half = inverse_ref.shape[0] // rows
    total = refs[-2][...] if more else jnp.zeros((wave_rows, rows), F32)
    for n, i in enumerate(blocks):
        place = pl.ds(pl.multiple_of(((chip % half) ^ i) * rows, rows), rows)
        total += jnp.dot(refs[n][...], inverse_ref[place, :], preferred_element_type=F32)
    out_ref[...] = total.astype(out_ref.dtype)


def join_kernel(
    turn, mine_ref, other_ref, state_ref, scale_ref, later_ref, next_ref, out_ref
):
    wave_rows = mine_ref.shape[0]
    last = lax.axis_index("panel") == lax.axis_size("panel") - 1
    forward, backward, wave = own_turn(turn)
    here = pl.ds(pl.multiple_of(wave * wave_rows, wave_rows), wave_rows)
    solved = (mine_ref[...].astype(F32) + other_ref[...].astype(F32)).astype(BF16).astype(F32)
    older = state_ref[here, :].astype(F32)
    field = (solved + jnp.where(backward, older, 0.0)).astype(BF16)
    scale = jnp.where(backward, scale_ref[1:2, :], scale_ref[0:1, :])
    ahead = jnp.where(forward & ~last, later_ref[here, :].astype(F32), 0.0)
    out_ref[...] = (scale * field.astype(F32) + ahead).astype(BF16)
    if turn == 0:

        @pl.when(last)
        def _():
            out_ref[...] = later_ref[wave_rows : 2 * wave_rows, :]

    @pl.when(forward | backward)
    def _():
        next_ref[here, :] = field


def last_join_kernel(turn, mine_ref, other_ref, state_ref, next_ref, top_ref):
    wave_rows = mine_ref.shape[0]
    rows = top_ref.shape[1]
    forward, backward, wave = own_turn(turn)
    here = pl.ds(pl.multiple_of(wave * wave_rows, wave_rows), wave_rows)
    solved = (mine_ref[...].astype(F32) + other_ref[...].astype(F32)).astype(BF16).astype(F32)
    older = state_ref[here, :].astype(F32)

    @pl.when(forward | backward)
    def _():
        next_ref[here, :] = (solved + jnp.where(backward, older, 0.0)).astype(BF16)

    @pl.when(own_place()[1] == 0)
    def _():
        top_ref[...] = next_ref[:, :rows]

    @pl.when(own_place()[1] != 0)
    def _():
        top_ref[...] = next_ref[:, rows:]


def turn_routes(turn, panels, waves):
    if turn == 0:
        return [(p, (p + 1) % panels) for p in range(panels)]
    at = [s if s < panels else 2 * (panels - 1) - s for s in range(2 * panels - 1)]
    pairs = []
    for wave in range(waves):
        step = turn - wave
        if 0 <= step < 2 * (panels - 1):
            pairs.append((at[step], at[step + 1]))
    sources = [a for a, _ in pairs]
    targets = [b for _, b in pairs]
    for panel in range(panels):
        if panel not in sources and panel not in targets:
            pairs.append((panel, panel))
    spare = [p for p in targets if p not in sources]
    unfed = [p for p in sources if p not in targets]
    return pairs + list(zip(spare, unfed))


def preparing_turns(panels):
    turns = range(1, 2 * (panels - 1) + WAVES - 1)
    alone = {t: [p for p, q in turn_routes(t, panels, WAVES) if p == q] for t in turns}
    chosen = {}
    left = list(range(panels))
    while left:
        turn = max(turns, key=lambda t: sum(p in left for p in alone[t]))
        found = [p for p in left if p in alone[turn]] or left
        chosen[turn] = chosen.get(turn, []) + found
        left = [p for p in left if p not in found]
    return chosen


def spread(values, panel_pairs, chips):
    half = chips // 2
    received = []
    for i in reversed(range(half)):
        route = []
        for start, end in panel_pairs:
            for chip in range(chips):
                for core in range(2):
                    there = chip ^ (half * core + i)
                    route.append(
                        (2 * (start * chips + chip) + core, 2 * (end * chips + there) + core)
                    )
        received.append(lax.ppermute(values, ("panel", "front"), route))
    return received[::-1]


def body(top_source, leaf_source, top_inverse, leaf_inverse, boundary, touch_rows, coupling):
    sources = top_source.shape[1]
    rows = top_source.shape[2]
    width = top_inverse.shape[2]
    leaf_count, leaf_size = leaf_inverse.shape[1:3]
    edge = boundary.shape[2]
    panels = lax.axis_size("panel")
    front = lax.axis_size("front")
    chips, half = front // 2, front // 4
    chip_rows = 2 * rows
    panel = lax.axis_index("panel")
    core = lax.axis_index("front") % 2
    wave_rows = sources // WAVES
    group = group_of(leaf_count, 6)
    steps = leaf_count // group
    all_lanes = leaf_count * leaf_size

    swap_core = [(i, i ^ 1) for i in range(front)]
    swap_chip = [(i, i + 1) for i in range(1, front - 1, 2)]
    swap_chip = swap_chip + [(j, i) for i, j in swap_chip]

    tile = group_of(leaf_count, 8 if leaf_count % 8 == 0 else 4)
    touch_rows = touch_rows.reshape(leaf_count // tile, tile, edge)
    pieces = group_of(rows // 16, 8)
    outward, partial, interior, given = pl.pallas_call(
        functools.partial(push_kernel, group),
        out_shape=(
            pltpu.VMEM((sources, rows), BF16),
            pltpu.VMEM((sources, chip_rows), F32),
            pltpu.VMEM((sources, all_lanes), BF16),
            pltpu.VMEM((rows, width // 2), BF16),
        ),
        in_specs=[VMEM] + [ANY] * 4,
        out_specs=(VMEM, VMEM, VMEM, VMEM),
        scratch_shapes=[
            pltpu.VMEM((sources, all_lanes), BF16),
            pltpu.VMEM((leaf_count, leaf_size, leaf_size), BF16),
            pltpu.VMEM((leaf_count, edge, leaf_size), BF16),
            pltpu.VMEM((2, group * edge, 3 * rows), BF16),
            pltpu.VMEM((sources, 3 * rows), F32),
            pltpu.SemaphoreType.DMA((half, pieces)),
            pltpu.SemaphoreType.DMA((steps, 3)),
        ],
        compiler_params=params(24),
    )(
        touch_rows,
        in_hbm(leaf_source[0]),
        in_hbm(leaf_inverse[0]),
        in_hbm(boundary[0]),
        in_hbm(top_inverse[0]),
    )
    coupling, given, outward = lax.optimization_barrier((coupling, given, outward))
    taken = lax.ppermute(given, "front", swap_core)
    inward = lax.ppermute(outward, "front", swap_chip)
    ring = [((p + 1) % panels, p) for p in range(panels)]
    later = lax.ppermute(coupling, "panel", ring)
    inward, later = lax.optimization_barrier((inward, later))
    forward_scale = jnp.where(panel == panels - 1, coupling, later)
    scales = jnp.concatenate([forward_scale, coupling], axis=0)
    own_part = top_source[0].astype(F32) - inward.astype(F32)
    blank = jnp.zeros_like(own_part)
    own_part = jnp.where(
        core == 0,
        jnp.concatenate([own_part, blank], axis=1),
        jnp.concatenate([blank, own_part], axis=1),
    )
    partial = (own_part - partial).astype(BF16)
    partner = lax.ppermute(partial, "front", swap_core)
    partner_scales = lax.ppermute(scales, "front", swap_core)
    known = (partial.astype(F32) + partner.astype(F32)).astype(BF16)
    scales = jnp.where(
        core == 0,
        jnp.concatenate([scales, partner_scales], axis=1),
        jnp.concatenate([partner_scales, scales], axis=1),
    )
    scales = in_vmem(scales)
    arrived = [in_vmem(a) for a in spread(known[:wave_rows], [(0, 0)], chips)]
    later_known = in_vmem(lax.ppermute(known, "panel", ring))

    inverse = pl.pallas_call(
        turn_kernel,
        out_shape=pltpu.VMEM((width // 2, chip_rows), BF16),
        in_specs=[ANY, ANY],
        out_specs=VMEM,
        scratch_shapes=[
            pltpu.VMEM((rows, width // 2), BF16),
            pltpu.VMEM((rows, width // 2), BF16),
            pltpu.SemaphoreType.DMA((half, pieces)),
            pltpu.SemaphoreType.DMA((half,)),
        ],
        compiler_params=params(8),
        cost_estimate=pl.CostEstimate(
            flops=2 * sources * width * rows, bytes_accessed=4 * width * rows, transcendentals=0
        ),
    )(in_hbm(top_inverse[0]), taken)
    inverse = in_vmem(inverse)

    state = jnp.zeros((sources, chip_rows), BF16)
    turns = 2 * (panels - 1) + WAVES
    extra, made = [], []
    preparing = preparing_turns(panels)
    for turn in range(turns):
        share = ()
        halves = (range(half // 2, half), range(half // 2))
        for blocks in halves:
            last = blocks is halves[-1]
            behind = extra if last else []
            operands = [arrived[i] for i in blocks] + [in_vmem(v) for v in share]
            share = (
                pl.pallas_call(
                    functools.partial(fold_kernel, blocks, bool(share), len(behind)),
                    out_shape=pltpu.VMEM((wave_rows, chip_rows), BF16 if last else F32),
                    in_specs=[VMEM] + [ANY] * len(behind) + [VMEM] * len(operands),
                    out_specs=VMEM,
                    compiler_params=params(4),
                )(inverse, *behind, *operands),
            )
        share, extra = share[0], []
        other = lax.ppermute(share, "front", swap_core)
        if turn == turns - 1:
            state, top_field = pl.pallas_call(
                functools.partial(last_join_kernel, turn),
                out_shape=(
                    pltpu.VMEM((sources, chip_rows), BF16),
                    pltpu.VMEM((sources, rows), BF16),
                ),
                in_specs=[VMEM] * 3,
                out_specs=(VMEM, VMEM),
                input_output_aliases={2: 0},
                compiler_params=params(4),
            )(in_vmem(share), in_vmem(other), in_vmem(state))
            break
        state, outgoing = pl.pallas_call(
            functools.partial(join_kernel, turn),
            out_shape=(
                pltpu.VMEM((sources, chip_rows), BF16),
                pltpu.VMEM((wave_rows, chip_rows), BF16),
            ),
            in_specs=[VMEM] * 5,
            out_specs=(VMEM, VMEM),
            input_output_aliases={2: 0},
            compiler_params=params(4),
        )(in_vmem(share), in_vmem(other), in_vmem(state), scales, later_known)
        routes = turn_routes(turn, panels, WAVES)
        arrived = [in_vmem(a) for a in spread(outgoing, routes, chips)]
        if turn in preparing:
            made = pl.pallas_call(
                functools.partial(prepare_kernel, group, preparing[turn], len(made)),
                out_shape=(
                    pltpu.VMEM((3 * rows, leaf_count * edge), BF16),
                    pltpu.VMEM((leaf_count, edge, leaf_size), BF16),
                ),
                in_specs=[VMEM] + [ANY] * (3 + len(made)),
                out_specs=(VMEM, VMEM),
                input_output_aliases={4 + i: i for i in range(len(made))},
                scratch_shapes=[
                    pltpu.VMEM((leaf_count, leaf_size, leaf_size), BF16),
                    pltpu.VMEM((leaf_count, edge, leaf_size), BF16),
                    pltpu.SemaphoreType.DMA((steps, 2)),
                ],
                compiler_params=params(12),
                cost_estimate=pl.CostEstimate(
                    flops=8 * sources * rows * leaf_count * edge,
                    bytes_accessed=6 * rows * leaf_count * edge,
                    transcendentals=0,
                ),
            )(touch_rows, in_hbm(leaf_inverse[0]), in_hbm(boundary[0]), outgoing, *made)
            made = [in_vmem(m) for m in made]
            extra = made
    picks, matrices = made

    beside = lax.ppermute(top_field, "front", swap_chip)
    picked = pl.pallas_call(
        near_kernel,
        out_shape=pltpu.VMEM((sources, leaf_count * edge), BF16),
        in_specs=[VMEM] * 2,
        out_specs=VMEM,
        compiler_params=params(8),
        cost_estimate=pl.CostEstimate(
            flops=4 * sources * rows * leaf_count * edge,
            bytes_accessed=4 * rows * leaf_count * edge,
            transcendentals=0,
        ),
    )(in_vmem(state), in_vmem(picks))
    leaf_field, top_field = pl.pallas_call(
        functools.partial(leaf_kernel, group),
        out_shape=(
            jax.ShapeDtypeStruct((sources, all_lanes), BF16),
            jax.ShapeDtypeStruct((sources, rows), BF16),
        ),
        in_specs=[VMEM] * 6,
        out_specs=(ANY, ANY),
        scratch_shapes=[
            pltpu.VMEM((sources, leaf_count * edge), BF16),
            pltpu.VMEM((sources, all_lanes), BF16),
            pltpu.SemaphoreType.DMA,
            pltpu.SemaphoreType.DMA((steps,)),
        ],
        compiler_params=params(8),
    )(in_vmem(beside), in_vmem(picked), in_vmem(picks), in_vmem(matrices), in_vmem(interior), in_vmem(top_field))
    return (top_field[None], leaf_field[None])


def solution(mesh):
    placed = (
        P("panel", None, "front"),
        P("panel", None, "front"),
        P("panel", "front", None),
        P("panel", "front", None, None),
        P("panel", "front", None, None),
        P("panel", "front", None),
        P("panel", "front"),
    )
    return jax.shard_map(
        body,
        mesh=mesh,
        in_specs=placed,
        out_specs=(P("panel", None, "front"), P("panel", None, "front")),
        check_vma=False,
    )
```

```python
import functools

import jax
import jax.numpy as jnp
from jax import lax
from jax.experimental import pallas as pl
from jax.experimental.pallas import tpu as pltpu
from jax.sharding import PartitionSpec as P

WAVES = 2
F32 = jnp.float32
BF16 = jnp.bfloat16
VMEM = pl.BlockSpec(memory_space=pltpu.VMEM)
ANY = pl.BlockSpec(memory_space=pl.ANY)


def params(mib):
    return pltpu.CompilerParams(vmem_limit_bytes=mib * 1024 * 1024)


def in_vmem(value):
    return pltpu.with_memory_space_constraint(value, pltpu.VMEM)


def in_hbm(value):
    return pltpu.with_memory_space_constraint(value, pltpu.HBM)


def rows_dot(left, right):
    return lax.dot_general(left, right, (((1,), (1,)), ((), ())), preferred_element_type=F32)


def group_of(leaf_count, most):
    return max(g for g in range(1, most + 1) if leaf_count % g == 0)


def own_place():
    place = lax.axis_index("front")
    return place // 2, place % 2


def own_half():
    chip, core = own_place()
    return (chip // (lax.axis_size("front") // 4)) ^ core


def own_turn(turn):
    panel = lax.axis_index("panel")
    panels = lax.axis_size("panel")
    up_wave = turn - panel
    down_wave = turn - (2 * (panels - 1) - panel)
    up = (up_wave >= 0) & (up_wave < WAVES)
    down = (down_wave >= 0) & (down_wave < WAVES) & (panel < panels - 1)
    wave = jnp.where(up, up_wave, jnp.where(down, down_wave, 0))
    return up, down, wave


def push_kernel(
    group,
    rows_ref,
    source_hbm,
    inverse_hbm,
    boundary_hbm,
    solver_hbm,
    outward_ref,
    partial_ref,
    interior_ref,
    given_ref,
    source_ref,
    inverse_ref,
    boundary_ref,
    pick_ref,
    total_ref,
    half_sems,
    sems,
):
    leaf_count, leaf_size = inverse_ref.shape[:2]
    edge = boundary_ref.shape[1]
    rows = outward_ref.shape[1]
    window = 3 * rows
    core = own_place()[1]
    copies = []
    for step in range(leaf_count // group):
        leaves = pl.ds(step * group, group)
        lanes = pl.ds(step * group * leaf_size, group * leaf_size)
        parts = (
            (source_hbm.at[:, lanes], source_ref.at[:, lanes]),
            (inverse_hbm.at[leaves], inverse_ref.at[leaves]),
            (boundary_hbm.at[leaves], boundary_ref.at[leaves]),
        )
        copies.append(
            [pltpu.make_async_copy(a, b, sems.at[step, i]) for i, (a, b) in enumerate(parts)]
        )
        for copy in copies[-1]:
            copy.start()
    staged = sum(half_copies(1 - own_half(), solver_hbm, given_ref, half_sems), [])
    places = lax.broadcasted_iota(jnp.int16, (edge, window), 1)
    for step in range(leaf_count // group):
        for copy in copies[step]:
            copy.wait()
        first = step * group
        interior = []
        for j in range(first, first + group):
            lanes = slice(j * leaf_size, (j + 1) * leaf_size)
            interior.append(rows_dot(source_ref[:, lanes], inverse_ref[j]).astype(BF16))
            interior_ref[:, lanes] = interior[-1]
        pushed = [
            rows_dot(interior[g], boundary_ref[first + g]).astype(BF16) for g in range(group)
        ]
        if step == 0:
            lines = [rows_ref[i] for i in range(rows_ref.shape[0])]
            if leaf_count % 8:
                lines.append(jnp.zeros((-leaf_count % 8, edge), jnp.int32))
            local = jnp.concatenate(lines, axis=0) - (lax.axis_index("front") - 1) * rows
            columns = jnp.transpose(local).astype(jnp.int16)
        for g in range(group):
            pick_ref[step % 2, g * edge : (g + 1) * edge, :] = jnp.where(
                columns[:, first + g : first + g + 1] == places, jnp.bfloat16(1), jnp.bfloat16(0)
            )
        total = jnp.dot(
            jnp.concatenate(pushed, axis=1), pick_ref[step % 2], preferred_element_type=F32
        )
        if step == 0:
            total_ref[...] = total
        else:
            total_ref[...] += total
    for copy in staged:
        copy.wait()
    @pl.when(core == 0)
    def _():
        outward_ref[...] = total_ref[:, :rows].astype(BF16)
        partial_ref[...] = total_ref[:, rows:]

    @pl.when(core != 0)
    def _():
        outward_ref[...] = total_ref[:, 2 * rows :].astype(BF16)
        partial_ref[...] = total_ref[:, : 2 * rows]


def prepare_kernel(
    group, panels, given, rows_ref, inverse_hbm, boundary_hbm, after_ref, *refs
):
    picks_ref, matrix_ref, inverse_ref, boundary_ref, sems = refs[given:]
    tile, edge = rows_ref.shape[1:]
    leaf_count = rows_ref.shape[0] * tile
    window = picks_ref.shape[0]
    rows = window // 3
    panel = lax.axis_index("panel")
    place = lax.axis_index("front")
    chosen = panel == panels[0]
    for other in panels[1:]:
        chosen = chosen | (panel == other)

    @pl.when(chosen)
    def _():
        copies = []
        for step in range(leaf_count // group):
            leaves = pl.ds(step * group, group)
            parts = (
                (inverse_hbm.at[leaves], inverse_ref.at[leaves]),
                (boundary_hbm.at[leaves], boundary_ref.at[leaves]),
            )
            copies.append(
                [pltpu.make_async_copy(a, b, sems.at[step, i]) for i, (a, b) in enumerate(parts)]
            )
            for copy in copies[-1]:
                copy.start()
        local = rows_ref[...] - (place - 1) * rows
        shifted = jnp.where(local < rows, local + 2 * rows, local - rows)
        local = jnp.where(place % 2 == 0, shifted, local)
        places = lax.broadcasted_iota(jnp.int16, (window, edge), 0)
        for j in range(leaf_count):
            picks_ref[:, j * edge : (j + 1) * edge] = jnp.where(
                local[j // tile, j % tile : j % tile + 1, :].astype(jnp.int16) == places,
                jnp.bfloat16(1),
                jnp.bfloat16(0),
            )
        for step in range(leaf_count // group):
            for copy in copies[step]:
                copy.wait()
            for j in range(step * group, (step + 1) * group):
                matrix_ref[j] = rows_dot(boundary_ref[j], inverse_ref[j]).astype(BF16)


def near_kernel(state_ref, pick_ref, out_ref):
    out_ref[...] = jnp.dot(
        state_ref[...], pick_ref[: state_ref.shape[1], :], preferred_element_type=F32
    ).astype(BF16)


def leaf_kernel(
    group,
    ready_ref,
    last_ref,
    picked_ref,
    pick_ref,
    matrix_ref,
    interior_ref,
    top_ref,
    out_hbm,
    top_hbm,
    all_ref,
    out_ref,
    top_sem,
    sems,
):
    leaf_count, edge, leaf_size = matrix_ref.shape
    rows = last_ref.shape[1]
    copies = [pltpu.make_async_copy(top_ref, top_hbm, top_sem)]
    copies[0].start()
    beside = jnp.concatenate([ready_ref[...], last_ref[...]], axis=0)
    picked = jnp.dot(beside, pick_ref[2 * rows :, :], preferred_element_type=F32)
    all_ref[...] = (picked + picked_ref[...].astype(F32)).astype(BF16)
    for step in range(leaf_count // group):
        first = step * group
        for j in range(first, first + group):
            lanes = slice(j * leaf_size, (j + 1) * leaf_size)
            lifted = jnp.dot(
                all_ref[:, j * edge : (j + 1) * edge],
                matrix_ref[j],
                preferred_element_type=F32,
            )
            out_ref[:, lanes] = (interior_ref[:, lanes].astype(F32) - lifted).astype(BF16)
        lanes = pl.ds(first * leaf_size, group * leaf_size)
        copies.append(
            pltpu.make_async_copy(out_ref.at[:, lanes], out_hbm.at[:, lanes], sems.at[step])
        )
        copies[-1].start()
    for copy in copies:
        copy.wait()


def half_copies(which, inverse_hbm, to_ref, sems):
    pairs, pieces = sems.shape
    span = to_ref.shape[1] // pairs
    tall = to_ref.shape[0] // pieces
    copies = []
    for q in range(pairs):
        start = pl.multiple_of((pairs * which + q) * span, span)
        copies.append([])
        for r in range(pieces):
            here = pl.ds(r * tall, tall)
            copies[-1].append(
                pltpu.make_async_copy(
                    inverse_hbm.at[here, pl.ds(start, span)],
                    to_ref.at[here, pl.ds(q * span, span)],
                    sems.at[q, r],
                )
            )
            copies[-1][-1].start()
    return copies


def turn_kernel(inverse_hbm, taken_hbm, out_ref, kept_ref, taken_ref, kept_sems, taken_sems):
    core = own_place()[1]
    rows = taken_ref.shape[0]
    span = kept_ref.shape[1] // kept_sems.shape[0]
    taken_copies = []
    for q in range(taken_sems.shape[0]):
        lanes = pl.ds(q * span, span)
        taken_copies.append(
            pltpu.make_async_copy(taken_hbm.at[:, lanes], taken_ref.at[:, lanes], taken_sems.at[q])
        )
        taken_copies[-1].start()
    kept_copies = half_copies(own_half(), inverse_hbm, kept_ref, kept_sems)
    piece = min(span, 256)
    for q in range(len(kept_copies)):
        taken_copies[q].wait()
        for copy in kept_copies[q]:
            copy.wait()
        for k in range(q * span, (q + 1) * span, piece):
            kept = jnp.transpose(kept_ref[:, k : k + piece])
            taken = jnp.transpose(taken_ref[:, k : k + piece])

            @pl.when(core == 0)
            def _():
                out_ref[k : k + piece, :rows] = kept
                out_ref[k : k + piece, rows:] = taken

            @pl.when(core != 0)
            def _():
                out_ref[k : k + piece, :rows] = taken
                out_ref[k : k + piece, rows:] = kept


def fold_kernel(blocks, more, skipped, inverse_ref, *refs):
    refs = refs[skipped:]
    out_ref = refs[-1]
    wave_rows, rows = out_ref.shape
    chip = own_place()[0]
    half = inverse_ref.shape[0] // rows
    total = refs[-2][...] if more else jnp.zeros((wave_rows, rows), F32)
    for n, i in enumerate(blocks):
        place = pl.ds(pl.multiple_of(((chip % half) ^ i) * rows, rows), rows)
        total += jnp.dot(refs[n][...], inverse_ref[place, :], preferred_element_type=F32)
    out_ref[...] = total.astype(out_ref.dtype)


def join_kernel(
    turn, mine_ref, other_ref, state_ref, scale_ref, later_ref, next_ref, out_ref
):
    wave_rows = mine_ref.shape[0]
    last = lax.axis_index("panel") == lax.axis_size("panel") - 1
    forward, backward, wave = own_turn(turn)
    here = pl.ds(pl.multiple_of(wave * wave_rows, wave_rows), wave_rows)
    solved = (mine_ref[...].astype(F32) + other_ref[...].astype(F32)).astype(BF16).astype(F32)
    older = state_ref[here, :].astype(F32)
    field = (solved + jnp.where(backward, older, 0.0)).astype(BF16)
    scale = jnp.where(backward, scale_ref[1:2, :], scale_ref[0:1, :])
    ahead = jnp.where(forward & ~last, later_ref[here, :].astype(F32), 0.0)
    out_ref[...] = (scale * field.astype(F32) + ahead).astype(BF16)
    if turn == 0:

        @pl.when(last)
        def _():
            out_ref[...] = later_ref[wave_rows : 2 * wave_rows, :]

    @pl.when(forward | backward)
    def _():
        next_ref[here, :] = field


def last_join_kernel(turn, mine_ref, other_ref, state_ref, next_ref, top_ref):
    wave_rows = mine_ref.shape[0]
    rows = top_ref.shape[1]
    forward, backward, wave = own_turn(turn)
    here = pl.ds(pl.multiple_of(wave * wave_rows, wave_rows), wave_rows)
    solved = (mine_ref[...].astype(F32) + other_ref[...].astype(F32)).astype(BF16).astype(F32)
    older = state_ref[here, :].astype(F32)

    @pl.when(forward | backward)
    def _():
        next_ref[here, :] = (solved + jnp.where(backward, older, 0.0)).astype(BF16)

    @pl.when(own_place()[1] == 0)
    def _():
        top_ref[...] = next_ref[:, :rows]

    @pl.when(own_place()[1] != 0)
    def _():
        top_ref[...] = next_ref[:, rows:]


def turn_routes(turn, panels, waves):
    if turn == 0:
        return [(p, (p + 1) % panels) for p in range(panels)]
    at = [s if s < panels else 2 * (panels - 1) - s for s in range(2 * panels - 1)]
    pairs = []
    for wave in range(waves):
        step = turn - wave
        if 0 <= step < 2 * (panels - 1):
            pairs.append((at[step], at[step + 1]))
    sources = [a for a, _ in pairs]
    targets = [b for _, b in pairs]
    for panel in range(panels):
        if panel not in sources and panel not in targets:
            pairs.append((panel, panel))
    spare = [p for p in targets if p not in sources]
    unfed = [p for p in sources if p not in targets]
    return pairs + list(zip(spare, unfed))


def preparing_turns(panels):
    turns = range(1, 2 * (panels - 1) + WAVES - 1)
    alone = {t: [p for p, q in turn_routes(t, panels, WAVES) if p == q] for t in turns}
    chosen = {}
    left = list(range(panels))
    while left:
        turn = max(turns, key=lambda t: sum(p in left for p in alone[t]))
        found = [p for p in left if p in alone[turn]] or left
        chosen[turn] = chosen.get(turn, []) + found
        left = [p for p in left if p not in found]
    return chosen


def spread(values, panel_pairs, chips):
    half = chips // 2
    received = []
    for i in reversed(range(half)):
        route = []
        for start, end in panel_pairs:
            for chip in range(chips):
                for core in range(2):
                    there = chip ^ (half * core + i)
                    route.append(
                        (2 * (start * chips + chip) + core, 2 * (end * chips + there) + core)
                    )
        received.append(lax.ppermute(values, ("panel", "front"), route))
    return received[::-1]


def body(top_source, leaf_source, top_inverse, leaf_inverse, boundary, touch_rows, coupling):
    sources = top_source.shape[1]
    rows = top_source.shape[2]
    width = top_inverse.shape[2]
    leaf_count, leaf_size = leaf_inverse.shape[1:3]
    edge = boundary.shape[2]
    panels = lax.axis_size("panel")
    front = lax.axis_size("front")
    chips, half = front // 2, front // 4
    chip_rows = 2 * rows
    panel = lax.axis_index("panel")
    core = lax.axis_index("front") % 2
    wave_rows = sources // WAVES
    group = group_of(leaf_count, 6)
    steps = leaf_count // group
    all_lanes = leaf_count * leaf_size

    swap_core = [(i, i ^ 1) for i in range(front)]
    swap_chip = [(i, i + 1) for i in range(1, front - 1, 2)]
    swap_chip = swap_chip + [(j, i) for i, j in swap_chip]

    tile = group_of(leaf_count, 8 if leaf_count % 8 == 0 else 4)
    touch_rows = touch_rows.reshape(leaf_count // tile, tile, edge)
    pieces = group_of(rows // 16, 8)
    outward, partial, interior, given = pl.pallas_call(
        functools.partial(push_kernel, group),
        out_shape=(
            pltpu.VMEM((sources, rows), BF16),
            pltpu.VMEM((sources, chip_rows), F32),
            pltpu.VMEM((sources, all_lanes), BF16),
            pltpu.VMEM((rows, width // 2), BF16),
        ),
        in_specs=[VMEM] + [ANY] * 4,
        out_specs=(VMEM, VMEM, VMEM, VMEM),
        scratch_shapes=[
            pltpu.VMEM((sources, all_lanes), BF16),
            pltpu.VMEM((leaf_count, leaf_size, leaf_size), BF16),
            pltpu.VMEM((leaf_count, edge, leaf_size), BF16),
            pltpu.VMEM((2, group * edge, 3 * rows), BF16),
            pltpu.VMEM((sources, 3 * rows), F32),
            pltpu.SemaphoreType.DMA((half, pieces)),
            pltpu.SemaphoreType.DMA((steps, 3)),
        ],
        compiler_params=params(24),
    )(
        touch_rows,
        in_hbm(leaf_source[0]),
        in_hbm(leaf_inverse[0]),
        in_hbm(boundary[0]),
        in_hbm(top_inverse[0]),
    )
    coupling, given, outward = lax.optimization_barrier((coupling, given, outward))
    taken = lax.ppermute(given, "front", swap_core)
    inward = lax.ppermute(outward, "front", swap_chip)
    ring = [((p + 1) % panels, p) for p in range(panels)]
    later = lax.ppermute(coupling, "panel", ring)
    inward, later = lax.optimization_barrier((inward, later))
    forward_scale = jnp.where(panel == panels - 1, coupling, later)
    scales = jnp.concatenate([forward_scale, coupling], axis=0)
    own_part = top_source[0].astype(F32) - inward.astype(F32)
    blank = jnp.zeros_like(own_part)
    own_part = jnp.where(
        core == 0,
        jnp.concatenate([own_part, blank], axis=1),
        jnp.concatenate([blank, own_part], axis=1),
    )
    partial = (own_part - partial).astype(BF16)
    partner = lax.ppermute(partial, "front", swap_core)
    partner_scales = lax.ppermute(scales, "front", swap_core)
    known = (partial.astype(F32) + partner.astype(F32)).astype(BF16)
    scales = jnp.where(
        core == 0,
        jnp.concatenate([scales, partner_scales], axis=1),
        jnp.concatenate([partner_scales, scales], axis=1),
    )
    scales = in_vmem(scales)
    arrived = [in_vmem(a) for a in spread(known[:wave_rows], [(0, 0)], chips)]
    later_known = in_vmem(lax.ppermute(known, "panel", ring))

    inverse = pl.pallas_call(
        turn_kernel,
        out_shape=pltpu.VMEM((width // 2, chip_rows), BF16),
        in_specs=[ANY, ANY],
        out_specs=VMEM,
        scratch_shapes=[
            pltpu.VMEM((rows, width // 2), BF16),
            pltpu.VMEM((rows, width // 2), BF16),
            pltpu.SemaphoreType.DMA((half, pieces)),
            pltpu.SemaphoreType.DMA((half,)),
        ],
        compiler_params=params(8),
        cost_estimate=pl.CostEstimate(
            flops=2 * sources * width * rows, bytes_accessed=4 * width * rows, transcendentals=0
        ),
    )(in_hbm(top_inverse[0]), taken)
    inverse = in_vmem(inverse)

    state = jnp.zeros((sources, chip_rows), BF16)
    turns = 2 * (panels - 1) + WAVES
    extra, made = [], []
    preparing = preparing_turns(panels)
    for turn in range(turns):
        share = ()
        halves = (range(half // 2, half), range(half // 2))
        for blocks in halves:
            last = blocks is halves[-1]
            behind = extra if last else []
            operands = [arrived[i] for i in blocks] + [in_vmem(v) for v in share]
            share = (
                pl.pallas_call(
                    functools.partial(fold_kernel, blocks, bool(share), len(behind)),
                    out_shape=pltpu.VMEM((wave_rows, chip_rows), BF16 if last else F32),
                    in_specs=[VMEM] + [ANY] * len(behind) + [VMEM] * len(operands),
                    out_specs=VMEM,
                    compiler_params=params(4),
                )(inverse, *behind, *operands),
            )
        share, extra = share[0], []
        other = lax.ppermute(share, "front", swap_core)
        if turn == turns - 1:
            state, top_field = pl.pallas_call(
                functools.partial(last_join_kernel, turn),
                out_shape=(
                    pltpu.VMEM((sources, chip_rows), BF16),
                    pltpu.VMEM((sources, rows), BF16),
                ),
                in_specs=[VMEM] * 3,
                out_specs=(VMEM, VMEM),
                input_output_aliases={2: 0},
                compiler_params=params(4),
            )(in_vmem(share), in_vmem(other), in_vmem(state))
            break
        state, outgoing = pl.pallas_call(
            functools.partial(join_kernel, turn),
            out_shape=(
                pltpu.VMEM((sources, chip_rows), BF16),
                pltpu.VMEM((wave_rows, chip_rows), BF16),
            ),
            in_specs=[VMEM] * 5,
            out_specs=(VMEM, VMEM),
            input_output_aliases={2: 0},
            compiler_params=params(4),
        )(in_vmem(share), in_vmem(other), in_vmem(state), scales, later_known)
        if turn == turns - 2:
            ready = state[: sources - wave_rows]
            ready = jnp.where(core == 0, ready[:, :rows], ready[:, rows:])
            beside_ready = lax.ppermute(ready, "front", swap_chip)
        routes = turn_routes(turn, panels, WAVES)
        arrived = [in_vmem(a) for a in spread(outgoing, routes, chips)]
        if turn in preparing:
            made = pl.pallas_call(
                functools.partial(prepare_kernel, group, preparing[turn], len(made)),
                out_shape=(
                    pltpu.VMEM((3 * rows, leaf_count * edge), BF16),
                    pltpu.VMEM((leaf_count, edge, leaf_size), BF16),
                ),
                in_specs=[VMEM] + [ANY] * (3 + len(made)),
                out_specs=(VMEM, VMEM),
                input_output_aliases={4 + i: i for i in range(len(made))},
                scratch_shapes=[
                    pltpu.VMEM((leaf_count, leaf_size, leaf_size), BF16),
                    pltpu.VMEM((leaf_count, edge, leaf_size), BF16),
                    pltpu.SemaphoreType.DMA((steps, 2)),
                ],
                compiler_params=params(12),
                cost_estimate=pl.CostEstimate(
                    flops=8 * sources * rows * leaf_count * edge,
                    bytes_accessed=6 * rows * leaf_count * edge,
                    transcendentals=0,
                ),
            )(touch_rows, in_hbm(leaf_inverse[0]), in_hbm(boundary[0]), outgoing, *made)
            made = [in_vmem(m) for m in made]
            extra = made
    picks, matrices = made

    beside_last = lax.ppermute(top_field[sources - wave_rows :], "front", swap_chip)
    picked = pl.pallas_call(
        near_kernel,
        out_shape=pltpu.VMEM((sources, leaf_count * edge), BF16),
        in_specs=[VMEM] * 2,
        out_specs=VMEM,
        compiler_params=params(8),
        cost_estimate=pl.CostEstimate(
            flops=4 * sources * rows * leaf_count * edge,
            bytes_accessed=4 * rows * leaf_count * edge,
            transcendentals=0,
        ),
    )(in_vmem(state), in_vmem(picks))
    leaf_field, top_field = pl.pallas_call(
        functools.partial(leaf_kernel, group),
        out_shape=(
            jax.ShapeDtypeStruct((sources, all_lanes), BF16),
            jax.ShapeDtypeStruct((sources, rows), BF16),
        ),
        in_specs=[VMEM] * 7,
        out_specs=(ANY, ANY),
        scratch_shapes=[
            pltpu.VMEM((sources, leaf_count * edge), BF16),
            pltpu.VMEM((sources, all_lanes), BF16),
            pltpu.SemaphoreType.DMA,
            pltpu.SemaphoreType.DMA((steps,)),
        ],
        compiler_params=params(8),
    )(in_vmem(beside_ready), in_vmem(beside_last), in_vmem(picked), in_vmem(picks), in_vmem(matrices), in_vmem(interior), in_vmem(top_field))
    return (top_field[None], leaf_field[None])


def solution(mesh):
    placed = (
        P("panel", None, "front"),
        P("panel", None, "front"),
        P("panel", "front", None),
        P("panel", "front", None, None),
        P("panel", "front", None, None),
        P("panel", "front", None),
        P("panel", "front"),
    )
    return jax.shard_map(
        body,
        mesh=mesh,
        in_specs=placed,
        out_specs=(P("panel", None, "front"), P("panel", None, "front")),
        check_vma=False,
    )
```
